32 devices in a mesh: tm: 8 (over y, x, core), space: 4 (over z).
Axes of the slice: x: 2, y: 2, z: 4, core: 2. Of those that a mesh axis runs over, the one named last changes fastest.
Arguments:
- start: float32 [8, 2, 32, 64, 128], P('tm', None, 'space'), may hold values from -0.2 to 1.2
- conduct: float32 [32, 64, 128], P('space'), may hold values from 0.03 to 0.12
- threshold: float32 [32, 64, 128], P('space'), may hold values from 0.05 to 0.45
- recovery: float32 [32, 64, 128], P('space'), may hold values from 0.02 to 0.3
Outputs:
- final: float32 [8, 2, 32, 64, 128], P('tm', None, 'space')
The draws below stay inside these ranges and needn't reach their ends.
All inputs are finite; a program needn't handle non-finite values.
Results may differ from the reference program's by a relative error of at most 0.0001.
Values sent between devices are 32-bit elements; how exact they have to be, the bound alone decides.
A program may use at most 64 MiB of HBM per device.

```python
import math
import jax
import jax.numpy as jnp
from jax import lax

NY = 64
NZ = 128
ITERS = 2
SLICES = 8
NX = 32


def shard_levels(own_key, shape, split, smallest, high):
    def one(position, shards_of):
        draws = jax.random.uniform(jax.random.fold_in(jax.random.fold_in(own_key, 6), position), (shards_of,), jnp.float32, smallest / len(split), high / len(split))
        return jnp.repeat(jnp.exp(draws), shape[position] // shards_of).reshape((-1,) + (1,) * (len(shape) - position - 1))

    gain = one(*split[0])
    for cut in split[1:]:
        gain = gain * one(*cut)
    return gain


def setup_inputs(seed: int = 0) -> dict:
    streams_of = jax.random.split(jax.random.key(seed), 5)
    return {
        "start": jnp.clip(-0.2 + 1.4000001 * jax.random.uniform(streams_of[0], (SLICES, 2, NX, NY, NZ), jnp.float32) ** shard_levels(streams_of[0], (SLICES, 2, NX, NY, NZ), ((0, 8), (2, 4)), -0.2, 0.2), -0.2, 1.2),
        "conduct": jnp.clip(jnp.exp(math.log(0.12) - 1.3862944 * jax.random.uniform(streams_of[1], (NX, NY, NZ), jnp.float32) ** shard_levels(streams_of[1], (NX, NY, NZ), ((0, 4),), -0.2, 0.2)), 0.03, 0.12),
        "threshold": jnp.clip(0.05 + 0.39999999 * jax.random.uniform(streams_of[2], (NX, NY, NZ), jnp.float32) ** shard_levels(streams_of[2], (NX, NY, NZ), ((0, 4),), -0.2, 0.2), 0.05, 0.45),
        "recovery": jnp.clip(jnp.exp(math.log(0.3) - 2.7080503 * jax.random.uniform(streams_of[3], (NX, NY, NZ), jnp.float32) ** shard_levels(streams_of[3], (NX, NY, NZ), ((0, 4),), -0.2, 0.2)), 0.02, 0.3),
    }


quad_first = (5.0 / 24.0, 1.0 / 3.0, -1.0 / 24.0)
quad_second = (-1.0 / 24.0, 1.0 / 3.0, 5.0 / 24.0)
node_step = 0.5
reaction = 2.0
recovery_ratio = 0.5


def quadrature(weights, terms):
    return weights[0] * terms[0] + weights[1] * terms[1] + weights[2] * terms[2]


def fine_laplace(padded, values):
    summed = padded[:, 2:, 1:-1, 1:-1] + padded[:, :-2, 1:-1, 1:-1]
    summed = summed + padded[:, 1:-1, 2:, 1:-1] + padded[:, 1:-1, :-2, 1:-1]
    summed = summed + padded[:, 1:-1, 1:-1, 2:] + padded[:, 1:-1, 1:-1, :-2]
    return summed - 6.0 * values


def coarse_laplace(padded, values):
    along_x = padded[:, 2:, 1:-1, 1:-1] + padded[:, :-2, 1:-1, 1:-1] - 2.0 * values
    along_y = padded[:, 1:-1, 2:, 1:-1] + padded[:, 1:-1, :-2, 1:-1] - 2.0 * values
    along_z = padded[:, 1:-1, 1:-1, 2:] + padded[:, 1:-1, 1:-1, :-2] - 2.0 * values
    return 0.25 * along_x + 0.25 * along_y + along_z


def forces(states, laplace, coeffs):
    conduct, threshold, recovery = coeffs
    excite = states[:, 0]
    slower = states[:, 1]
    driving = conduct * laplace + reaction * excite * (1.0 - excite) * (excite - threshold) - slower
    relaxing = recovery * (excite - recovery_ratio * slower)
    return jnp.stack([driving, relaxing], axis=1)


def restrict(values):
    sizes_of = values.shape
    blocks = values.reshape(sizes_of[:-3] + (sizes_of[-3] // 2, 2, sizes_of[-2] // 2, 2, sizes_of[-1]))
    return 0.25 * jnp.sum(blocks, axis=(-4, -2))


def prolong(values):
    sizes_of = values.shape
    widened = jnp.broadcast_to(values[..., :, None, :, None, :], sizes_of[:-3] + (sizes_of[-3], 2, sizes_of[-2], 2, sizes_of[-1]))
    return widened.reshape(sizes_of[:-3] + (2 * sizes_of[-3], 2 * sizes_of[-2], sizes_of[-1]))


def fine_all(states, coeffs):
    padded = jnp.pad(states[:, 0], ((0, 0), (1, 1), (1, 1), (1, 1)))
    return forces(states, fine_laplace(padded, states[:, 0]), coeffs)


def coarse_all(states, coeffs):
    padded = jnp.pad(states[:, 0], ((0, 0), (1, 1), (1, 1), (1, 1)))
    return forces(states, coarse_laplace(padded, states[:, 0]), coeffs)


def slice_pass(nodes, initial, fine_coeffs, coarse_coeffs):
    old_terms = fine_all(nodes, fine_coeffs)
    term_zero = fine_all(initial[None], fine_coeffs)[0]
    node_one = initial + node_step * (term_zero - old_terms[0]) + quadrature(quad_first, old_terms)
    term_one = fine_all(node_one[None], fine_coeffs)[0]
    node_two = node_one + node_step * (term_one - old_terms[1]) + quadrature(quad_second, old_terms)
    term_two = fine_all(node_two[None], fine_coeffs)[0]
    new_terms = (term_zero, term_one, term_two)
    sum_first = quadrature(quad_first, new_terms)
    sum_second = quadrature(quad_second, new_terms)
    coarse_zero = restrict(initial)
    base_one = restrict(node_one)
    coarse_one = coarse_zero + restrict(sum_first)
    pair_terms = coarse_all(jnp.stack([base_one, coarse_one]), coarse_coeffs)
    coarse_two = coarse_one + node_step * (pair_terms[1] - pair_terms[0]) + restrict(sum_second)
    node_one_new = node_one + prolong(coarse_one - base_one)
    node_two_new = node_two + prolong(coarse_two - restrict(node_two))
    return jnp.stack([initial, node_one_new, node_two_new])


def reference(start, conduct, threshold, recovery):
    fine_coeffs = (conduct, threshold, recovery)
    coarse_coeffs = (restrict(conduct), restrict(threshold), restrict(recovery))
    nodes = jnp.broadcast_to(start[:, None], (SLICES, 3) + start.shape[1:])
    initials = start

    def one_slice(carried):
        return slice_pass(carried[0], carried[1], fine_coeffs, coarse_coeffs)

    for sweep_index in range(ITERS):
        nodes = lax.map(one_slice, (nodes, initials))
        initials = jnp.concatenate([start[:1], nodes[:-1, 2]], axis=0)
    return nodes[:, 2]
```

```python
import functools
import jax
import jax.numpy as jnp
from jax import lax
from jax.experimental import pallas as pl
from jax.experimental.pallas import tpu as pltpu
from jax.sharding import PartitionSpec as P

MESH = pl.DeviceIdType.MESH
SIXTH = 1.0 / 6.0
W24 = 1.0 / 24.0


def react(e, t):
    return 2.0 * e * (1.0 - e) * (e - t)


def near(v, axis, by):
    n = v.shape[axis]
    at = lax.broadcasted_iota(jnp.int32, v.shape, axis)
    low = jnp.where(at < by, 0.0, pltpu.roll(v, by, axis))
    high = jnp.where(at >= n - by, 0.0, pltpu.roll(v, n - by, axis))
    return low + high


def tiles(v, by):
    rows, lanes = v.shape
    return pltpu.roll(v.reshape(rows // 8, 8, lanes), by, 1).reshape(rows, lanes)


def even_rows(v):
    return lax.broadcasted_iota(jnp.int32, v.shape, 0) % 2 == 0


def pair(v):
    return v + jnp.where(even_rows(v), tiles(v, 7), tiles(v, 1))


def fold(v):
    half = v.shape[0] // 2
    return jnp.where(even_rows(v[:half]), v[:half], v[half:])


def expand(x):
    even = even_rows(x)
    return jnp.where(even, x, tiles(x, 1)), jnp.where(even, tiles(x, 7), x)


def unfold(x):
    return jnp.concatenate(expand(x), axis=0)


def inplane(e):
    return near(e, 0, 1) + near(e, 1, 1) - 6.0 * e


MESSAGES = {
    name: at
    for at, name in enumerate(
        [
            (kind, side)
            for kind in ("q", "c", "n1p", "n2", "dp", "n2x", "j", "jx", "m1", "m2p", "d2")
            for side in (0, 1)
        ]
        + ["n2r", "n2e", "jt"]
    )
}


def kernel(
    start, cond, thr, rec, out,
    qe, qr, c, t, k, cc, tc, kc,
    f0e, f0r, n1e, n1r, n2e, n2r, t1e, t1r,
    dE, dR, jE, jR, u1e, u2e, s1e, s1r, s2e, s2r,
    qne, qnr, m1e, m1r, m2e, m2r, t0e, t0r, oe, orr,
    n1s, n1h, ds, dh, js, jh, jxh, n2xh, rn2r, rn2e, jts, jth,
    m2s, m2h, d2s, d2h,
    load_sem, store_sem, send_sem, recv_sem,
):
    nx = qr.shape[0]
    cn = nx // 2
    p, s = lax.axis_index("tm"), lax.axis_index("space")
    slices, slabs = lax.axis_size("tm"), lax.axis_size("space")
    head = p == 0
    has = (s > 0, s < slabs - 1)
    earlier, later = p > 0, p < slices - 1
    plane = qe.shape[1:]
    zeros = jnp.zeros(plane, jnp.float32)

    loads = [
        pltpu.make_async_copy(src, dst, load_sem.at[i])
        for i, (src, dst) in enumerate(
            [
                (start.at[0, 0], qe.at[pl.ds(1, nx)]),
                (cond, c.at[pl.ds(1, nx)]),
                (thr, t),
                (start.at[0, 1], qr),
                (rec, k),
            ]
        )
    ]
    for load in loads:
        load.start()

    barrier = pltpu.get_barrier_semaphore()

    def greet(when, dp, dside):
        @pl.when(when)
        def _():
            pl.semaphore_signal(barrier, inc=1, device_id=(p + dp, s + dside), device_id_type=MESH)

    greet(has[0], 0, -1)
    greet(has[1], 0, 1)
    greet(earlier, -1, 0)
    greet(earlier & has[0], -1, -1)
    greet(earlier & has[1], -1, 1)

    for side in (0, 1):
        end = side * (nx + 1)

        @pl.when(jnp.logical_not(has[side]))
        def _():
            for ref in (qe, c):
                ref[end] = zeros
            for ref in (n1h, n2xh, m2h):
                ref[side] = zeros
            n2e[end] = zeros
            m1e[end] = zeros
            for ref in (dh, jh, jxh, d2h):
                ref[side] = zeros[: plane[0] // 2]

    sides = has[0].astype(jnp.int32) + has[1].astype(jnp.int32)
    after = later.astype(jnp.int32)
    pl.semaphore_wait(barrier, sides + after * (sides + 1))

    pending = []

    def copy_of(name, src, dst, dp, dside):
        at = MESSAGES[name]
        return pltpu.make_async_remote_copy(
            src_ref=src,
            dst_ref=dst,
            send_sem=send_sem.at[at],
            recv_sem=recv_sem.at[at],
            device_id=(p + dp, s + dside),
            device_id_type=MESH,
        )

    def send(name, src, dst, when, dp=0, dside=0):
        @pl.when(when)
        def _():
            copy_of(name, src, dst, dp, dside).start()

        pending.append((name, src, dst, when, dp, dside))

    def receive(name, dst, when):
        @pl.when(when)
        def _():
            copy_of(name, dst, dst, 0, 0).wait_recv()

    def to_sides(kind, src, dst):
        for side in (0, 1):
            send((kind, side), src(side), dst(1 - side), has[side], 0, 2 * side - 1)

    def to_later_sides(kind, src, dst):
        for side in (0, 1):
            send((kind, side), src(side), dst(1 - side), later & has[side], 1, 2 * side - 1)

    def from_side(kind, side, dst, when=None):
        receive((kind, 1 - side), dst, has[side] if when is None else when & has[side])

    def edge(side):
        return side * (nx - 1)

    def halo(ref):
        return lambda side: ref.at[side * (ref.shape[0] - 1)]

    def slot(ref):
        return lambda side: ref.at[side]

    def each(low, high, body):
        def step(i, _):
            body(i)
            return 0

        lax.fori_loop(low, high, step, 0)

    def on_edges(body):
        each(0, 2, lambda side: body(side, side * (nx - 1), 2 + side * (nx - 3)))

    to_sides("q", lambda side: start.at[0, 0, edge(side)], halo(qe))
    to_sides("c", lambda side: cond.at[edge(side)], halo(c))
    for load in loads:
        load.wait()

    def first_edge(side, i, inner):
        e, r = qe[i + 1], qr[i]
        f = c[i + 1] * (qe[inner] + inplane(e)) + react(e, t[i]) - r
        g = k[i] * (e - 0.5 * r)
        f0e[i], f0r[i] = f, g
        n1 = e + 0.5 * f
        n1e[i + 1], n1s[side], n1r[i] = n1, n1, r + 0.5 * g

    on_edges(first_edge)
    to_sides("n1p", slot(n1s), slot(n1h))

    def slow_step(i):
        g = k[i] * (n1e[i + 1] - 0.5 * n1r[i])
        t1r[i] = g
        n2r[i] = n1r[i] + 0.5 * g

    def first_inner(i):
        e, r = qe[i + 1], qr[i]
        f = c[i + 1] * (qe[i] + qe[i + 2] + inplane(e)) + react(e, t[i]) - r
        g = k[i] * (e - 0.5 * r)
        f0e[i], f0r[i] = f, g
        n1e[i + 1], n1r[i] = e + 0.5 * f, r + 0.5 * g
        slow_step(i)

    each(1, nx - 1, first_inner)

    def coarse_coeffs(j):
        for fine, shift, coarse in ((c, 1, cc), (t, 0, tc), (k, 0, kc)):
            coarse[j] = 0.25 * pair(fine[2 * j + shift] + fine[2 * j + 1 + shift])

    each(0, cn, coarse_coeffs)

    for side in (0, 1):
        i, end = edge(side), side * (nx + 1)
        from_side("q", side, qe.at[end])
        from_side("c", side, c.at[end])
        from_side("n1p", side, n1h.at[side])
        more = c[i + 1] * qe[end]
        f0e[i] += more
        n1e[i + 1] += 0.5 * more
        n1e[end] = n1h[side] + 0.5 * c[end] * qe[i + 1]
        slow_step(i)

    send("n2r", n2r, rn2r, later, 1)

    def second(i):
        e = n1e[i + 1]
        f = c[i + 1] * (n1e[i] + n1e[i + 2] + inplane(e)) + react(e, t[i]) - n1r[i]
        t1e[i] = f
        n2e[i + 1] = e + 0.5 * f

    on_edges(lambda side, i, inner: second(i))
    own_edge = lambda ref: lambda side: ref.at[edge(side) + 1]
    to_sides("n2", own_edge(n2e), halo(n2e))
    to_later_sides("n2x", own_edge(n2e), slot(n2xh))
    each(1, nx - 1, second)
    send("n2e", n2e.at[pl.ds(1, nx)], rn2e, later, 1)

    def third(j, e_ref, r_ref, extra, missing=None):
        sums = [0.0, 0.0, 0.0, 0.0]
        for row in (0, 1):
            i = 2 * j + row
            e, r = e_ref[i + 1], r_ref[i]
            if missing == 0 and row == 0:
                x = e_ref[i + 2]
            elif missing == 1 and row == 1:
                x = e_ref[i]
            else:
                x = e_ref[i] + e_ref[i + 2]
            fe = c[i + 1] * (x + inplane(e)) + react(e, t[i]) - r
            fr = k[i] * (e - 0.5 * r)
            a, b, g, h = extra(i)
            sums[0] += a - W24 * fe
            sums[1] += b - W24 * fr
            sums[2] += g + SIXTH * fe
            sums[3] += h + SIXTH * fr
        dE[j + 1] = 0.25 * pair(sums[0])
        dR[j] = 0.25 * pair(sums[1])
        jE[j] = 0.25 * pair(sums[2])
        jR[j] = 0.25 * pair(sums[3])

    def extra_first(i):
        a, b, g, h = f0e[i], t1e[i], f0r[i], t1r[i]
        return (
            8 * W24 * b - 7 * W24 * a,
            8 * W24 * h - 7 * W24 * g,
            SIXTH * b - 2 * SIXTH * a,
            SIXTH * h - 2 * SIXTH * g,
        )

    for side in (0, 1):
        third(side * (cn - 1), n2e, n2r, extra_first, side)
        ds[side] = fold(dE[side * (cn - 1) + 1])
    to_sides("dp", slot(ds), slot(dh))
    each(1, cn - 1, lambda j: third(j, n2e, n2r, extra_first))

    for side in (0, 1):
        i, j, end = edge(side), side * (cn - 1), side * (nx + 1)
        from_side("n2", side, n2e.at[end])
        from_side("dp", side, dh.at[side])
        more = 0.25 * pair(c[i + 1] * n2e[end])
        dE[j + 1] -= W24 * more
        jE[j] += SIXTH * more
        dE[side * (cn + 1)] = unfold(dh[side]) - (0.25 * W24) * pair(c[end] * n2e[i + 1])

    def coarse_step(j, node, x):
        d, dr = dE[j + 1], dR[j]
        lap = 0.25 * (x + near(d, 0, 2)) + near(d, 1, 1) - 3.0 * d
        b = 0.25 * pair(node[2 * j + 1] + node[2 * j + 2])
        return 0.5 * (cc[j] * lap + react(b + d, tc[j]) - react(b, tc[j]) - dr)

    def coarse_slow(j):
        return jR[j] + 0.5 * kc[j] * (dE[j + 1] - 0.5 * dR[j])

    def coarse_first(j):
        e = jE[j] + coarse_step(j, n1e, dE[j] + dE[j + 2])
        r = coarse_slow(j)
        jE[j], jR[j] = e, r
        jts[j] = jnp.where(even_rows(e), e, r)

    each(0, 2, lambda side: coarse_first(side * (cn - 1)))
    for side in (0, 1):
        js[side] = fold(jE[side * (cn - 1)])
    to_sides("j", slot(js), slot(jh))
    to_later_sides("jx", slot(js), slot(jxh))
    each(1, cn - 1, coarse_first)
    send("jt", jts, jth, later, 1)

    def correct(j):
        for row in (0, 1):
            i = 2 * j + row
            u1e[i + 1] = n1e[i + 1] + dE[j + 1]
            u2e[i + 1] = n2e[i + 1] + jE[j]

    each(0, cn, correct)
    for side in (0, 1):
        end = side * (nx + 1)
        u1e[end] = n1e[end] + dE[side * (cn + 1)]
        u2e[end] = zeros

    def old_terms(j):
        for row in (0, 1):
            i = 2 * j + row
            u1, u2 = u1e[i + 1], u2e[i + 1]
            u1r, u2r = n1r[i] + dR[j], n2r[i] + jR[j]
            a1 = c[i + 1] * (u1e[i] + u1e[i + 2] + inplane(u1)) + react(u1, t[i]) - u1r
            a2 = c[i + 1] * (u2e[i] + u2e[i + 2] + inplane(u2)) + react(u2, t[i]) - u2r
            b1 = k[i] * (u1 - 0.5 * u1r)
            b2 = k[i] * (u2 - 0.5 * u2r)
            a0, b0 = f0e[i], f0r[i]
            s1e[i] = 8 * W24 * a1 - 7 * W24 * a0 - W24 * a2
            s1r[i] = 8 * W24 * b1 - 7 * W24 * b0 - W24 * b2
            s2e[i] = 5 * W24 * a2 - W24 * a0 - 4 * W24 * a1
            s2r[i] = 5 * W24 * b2 - W24 * b0 - 4 * W24 * b1

    each(0, cn, old_terms)

    for side in (0, 1):
        i, end = edge(side), side * (nx + 1)
        from_side("j", side, jh.at[side])
        more = c[i + 1] * (n2e[end] + unfold(jh[side]))
        s1e[i] -= W24 * more
        s2e[i] += 5 * W24 * more

    receive("n2r", rn2r, earlier)
    receive("n2e", rn2e, earlier)
    for side in (0, 1):
        from_side("n2x", side, n2xh.at[side], earlier)
        from_side("jx", side, jxh.at[side], earlier)
        end = side * (nx + 1)
        qne[end] = jnp.where(head, qe[end], n2xh[side] + unfold(jxh[side]))
    receive("jt", jth, earlier)

    def arrive(j):
        e, r = expand(jth[j])
        for row in (0, 1):
            i = 2 * j + row
            qne[i + 1] = jnp.where(head, qe[i + 1], rn2e[i] + e)
            qnr[i] = jnp.where(head, qr[i], rn2r[i] + r)

    each(0, cn, arrive)

    def next_first(i):
        e, r = qne[i + 1], qnr[i]
        f = c[i + 1] * (qne[i] + qne[i + 2] + inplane(e)) + react(e, t[i]) - r
        g = k[i] * (e - 0.5 * r)
        t0e[i], t0r[i] = f, g
        m1e[i + 1] = e + 0.5 * f + s1e[i]
        m1r[i] = r + 0.5 * g + s1r[i]

    on_edges(lambda side, i, inner: next_first(i))
    to_sides("m1", own_edge(m1e), halo(m1e))
    on_edges(lambda side, i, inner: next_first(inner - 1))

    def next_second(i, x):
        e, r = m1e[i + 1], m1r[i]
        f = c[i + 1] * (x + inplane(e)) + react(e, t[i]) - r
        g = k[i] * (e - 0.5 * r)
        t1e[i], t1r[i] = f, g
        m2 = e + 0.5 * f + s2e[i]
        m2e[i + 1] = m2
        m2r[i] = r + 0.5 * g + s2r[i]
        return m2

    def next_edge(side, i, inner):
        m2s[side] = next_second(i, m1e[inner])

    on_edges(next_edge)
    to_sides("m2p", slot(m2s), slot(m2h))
    each(2, nx - 2, next_first)
    each(1, nx - 1, lambda i: next_second(i, m1e[i] + m1e[i + 2]))

    for side in (0, 1):
        i, end = edge(side), side * (nx + 1)
        from_side("m1", side, m1e.at[end])
        from_side("m2p", side, m2h.at[side])
        more = c[i + 1] * m1e[end]
        t1e[i] += more
        m2e[i + 1] += 0.5 * more
        m2e[end] = m2h[side] + 0.5 * c[end] * m1e[i + 1]

    def extra_next(i):
        a, b, g, h = t0e[i], t1e[i], t0r[i], t1r[i]
        return (
            8 * W24 * b - 7 * W24 * a - s1e[i],
            8 * W24 * h - 7 * W24 * g - s1r[i],
            SIXTH * b - 2 * SIXTH * a - s1e[i] - s2e[i],
            SIXTH * h - 2 * SIXTH * g - s1r[i] - s2r[i],
        )

    each(0, 2, lambda side: third(side * (cn - 1), m2e, m2r, extra_next))
    for side in (0, 1):
        d2s[side] = fold(dE[side * (cn - 1) + 1])
    to_sides("d2", slot(d2s), slot(d2h))
    each(1, cn - 1, lambda j: third(j, m2e, m2r, extra_next))

    def final_slow(j):
        r = coarse_slow(j)
        for row in (0, 1):
            orr[2 * j + row] = m2r[2 * j + row] + r

    each(0, cn, final_slow)
    stores = [pltpu.make_async_copy(orr, out.at[0, 1], store_sem.at[0])]
    stores[-1].start()

    def final_fast(j):
        e = jE[j] + coarse_step(j, m1e, dE[j] + dE[j + 2])
        for row in (0, 1):
            oe[2 * j + row] = m2e[2 * j + 1 + row] + e

    each(1, cn - 1, final_fast)
    if cn > 2:
        inside = pl.ds(2, nx - 4)
        stores.append(pltpu.make_async_copy(oe.at[inside], out.at[0, 0, inside], store_sem.at[1]))
        stores[-1].start()

    for side in (0, 1):
        j = side * (cn - 1)
        inner = dE[2 + side * (cn - 3)]
        e = jE[j] + coarse_step(j, m1e, inner)
        oe[2 * j] = m2e[2 * j + 1] + e
        oe[2 * j + 1] = m2e[2 * j + 2] + e
    for side in (0, 1):
        j = side * (cn - 1)
        from_side("d2", side, d2h.at[side])
        e = 0.125 * cc[j] * unfold(d2h[side])
        oe[2 * j] += e
        oe[2 * j + 1] += e
        rows = pl.ds(2 * j, 2)
        stores.append(
            pltpu.make_async_copy(oe.at[rows], out.at[0, 0, rows], store_sem.at[2 + side])
        )
        stores[-1].start()

    for name, src, dst, when, dp, dside in pending:

        @pl.when(when)
        def _():
            copy_of(name, src, dst, dp, dside).wait_send()

    for store in stores:
        store.wait()


def per_device(start, conduct, threshold, recovery):
    nx, ny, nz = conduct.shape
    cn = nx // 2

    def planes(count, rows=ny):
        return pltpu.VMEM((count, rows, nz), jnp.float32)

    own, padded, coarse, two, half = (
        planes(nx), planes(nx + 2), planes(cn), planes(2), planes(2, ny // 2)
    )
    scratch = [
        padded, own, padded, own, own, coarse, coarse, coarse,
        own, own, padded, own, padded, own, own, own,
        planes(cn + 2), coarse, coarse, coarse, padded, padded, own, own, own, own,
        padded, own, padded, own, padded, own, own, own, own, own,
        two, two, half, half, half, half, half, two, own, own, coarse, coarse,
        two, two, half, half,
        pltpu.SemaphoreType.DMA((5,)),
        pltpu.SemaphoreType.DMA((4,)),
        pltpu.SemaphoreType.DMA((len(MESSAGES),)),
        pltpu.SemaphoreType.DMA((len(MESSAGES),)),
    ]
    return pl.pallas_call(
        kernel,
        out_shape=jax.ShapeDtypeStruct(start.shape, jnp.float32),
        in_specs=[pl.BlockSpec(memory_space=pl.ANY)] * 4,
        out_specs=pl.BlockSpec(memory_space=pl.ANY),
        scratch_shapes=scratch,
        compiler_params=pltpu.CompilerParams(
            collective_id=0, has_side_effects=True, vmem_limit_bytes=48 * 1024 * 1024
        ),
    )(start, conduct, threshold, recovery)


def solution(mesh):
    placed = (
        P("tm", None, "space", None, None),
        P("space", None, None),
        P("space", None, None),
        P("space", None, None),
    )
    return jax.shard_map(
        per_device,
        mesh=mesh,
        in_specs=placed,
        out_specs=P("tm", None, "space", None, None),
        check_vma=False,
    )
```

```python
import functools
import jax
import jax.numpy as jnp
from jax import lax
from jax.experimental import pallas as pl
from jax.experimental.pallas import tpu as pltpu
from jax.sharding import PartitionSpec as P

MESH = pl.DeviceIdType.MESH
SIXTH = 1.0 / 6.0
W24 = 1.0 / 24.0


def react(e, t):
    return 2.0 * e * (1.0 - e) * (e - t)


def near(v, axis, by):
    n = v.shape[axis]
    at = lax.broadcasted_iota(jnp.int32, v.shape, axis)
    low = jnp.where(at < by, 0.0, pltpu.roll(v, by, axis))
    high = jnp.where(at >= n - by, 0.0, pltpu.roll(v, n - by, axis))
    return low + high


def tiles(v, by):
    rows, lanes = v.shape
    return pltpu.roll(v.reshape(rows // 8, 8, lanes), by, 1).reshape(rows, lanes)


def even_rows(v):
    return lax.broadcasted_iota(jnp.int32, v.shape, 0) % 2 == 0


def pair(v):
    return v + jnp.where(even_rows(v), tiles(v, 7), tiles(v, 1))


def fold(v):
    half = v.shape[0] // 2
    return jnp.where(even_rows(v[:half]), v[:half], v[half:])


def expand(x):
    even = even_rows(x)
    return jnp.where(even, x, tiles(x, 1)), jnp.where(even, tiles(x, 7), x)


def unfold(x):
    return jnp.concatenate(expand(x), axis=0)


def inplane(e):
    return near(e, 0, 1) + near(e, 1, 1) - 6.0 * e


MESSAGES = {
    name: at
    for at, name in enumerate(
        [
            (kind, side)
            for kind in ("q", "c", "n1p", "n2", "dp", "n2x", "j", "jx", "m1", "m2p", "d2")
            for side in (0, 1)
        ]
        + [(kind, side) for kind in ("n2r", "n2e") for side in (0, 1, 2)]
        + ["jt"]
    )
}


def kernel(
    start, cond, thr, rec, out,
    qe, qr, c, t, k, cc, tc, kc,
    f0e, f0r, n1e, n1r, n2e, n2r, t1e, t1r,
    dE, dR, jE, jR, u1e, u2e, s1e, s1r, s2e, s2r,
    qne, qnr, m1e, m1r, m2e, m2r, t0e, t0r, oe, orr,
    n1s, n1h, ds, dh, js, jh, jxh, n2xh, rn2r, rn2e, jts, jth,
    m2s, m2h, d2s, d2h,
    load_sem, store_sem, send_sem, recv_sem,
):
    nx = qr.shape[0]
    cn = nx // 2
    p, s = lax.axis_index("tm"), lax.axis_index("space")
    slices, slabs = lax.axis_size("tm"), lax.axis_size("space")
    head = p == 0
    has = (s > 0, s < slabs - 1)
    earlier, later = p > 0, p < slices - 1
    plane = qe.shape[1:]
    zeros = jnp.zeros(plane, jnp.float32)

    loads = [
        pltpu.make_async_copy(src, dst, load_sem.at[i])
        for i, (src, dst) in enumerate(
            [
                (start.at[0, 0], qe.at[pl.ds(1, nx)]),
                (cond, c.at[pl.ds(1, nx)]),
                (thr, t),
                (start.at[0, 1], qr),
                (rec, k),
            ]
        )
    ]
    for load in loads:
        load.start()

    barrier = pltpu.get_barrier_semaphore()

    def greet(when, dp, dside):
        @pl.when(when)
        def _():
            pl.semaphore_signal(barrier, inc=1, device_id=(p + dp, s + dside), device_id_type=MESH)

    greet(has[0], 0, -1)
    greet(has[1], 0, 1)
    greet(earlier, -1, 0)
    greet(earlier & has[0], -1, -1)
    greet(earlier & has[1], -1, 1)

    for side in (0, 1):
        end = side * (nx + 1)

        @pl.when(jnp.logical_not(has[side]))
        def _():
            for ref in (qe, c):
                ref[end] = zeros
            for ref in (n1h, n2xh, m2h):
                ref[side] = zeros
            n2e[end] = zeros
            m1e[end] = zeros
            for ref in (dh, jh, jxh, d2h):
                ref[side] = zeros[: plane[0] // 2]

    sides = has[0].astype(jnp.int32) + has[1].astype(jnp.int32)
    after = later.astype(jnp.int32)
    pl.semaphore_wait(barrier, sides + after * (sides + 1))

    pending = []

    def copy_of(name, src, dst, dp, dside):
        at = MESSAGES[name]
        return pltpu.make_async_remote_copy(
            src_ref=src,
            dst_ref=dst,
            send_sem=send_sem.at[at],
            recv_sem=recv_sem.at[at],
            device_id=(p + dp, s + dside),
            device_id_type=MESH,
        )

    def send(name, src, dst, when, dp=0, dside=0):
        @pl.when(when)
        def _():
            copy_of(name, src, dst, dp, dside).start()

        pending.append((name, src, dst, when, dp, dside))

    def receive(name, dst, when):
        @pl.when(when)
        def _():
            copy_of(name, dst, dst, 0, 0).wait_recv()

    def to_sides(kind, src, dst):
        for side in (0, 1):
            send((kind, side), src(side), dst(1 - side), has[side], 0, 2 * side - 1)

    def to_later_sides(kind, src, dst):
        for side in (0, 1):
            send((kind, side), src(side), dst(1 - side), later & has[side], 1, 2 * side - 1)

    def from_side(kind, side, dst, when=None):
        receive((kind, 1 - side), dst, has[side] if when is None else when & has[side])

    def edge(side):
        return side * (nx - 1)

    def halo(ref):
        return lambda side: ref.at[side * (ref.shape[0] - 1)]

    def slot(ref):
        return lambda side: ref.at[side]

    def each(low, high, body):
        def step(i, _):
            body(i)
            return 0

        lax.fori_loop(low, high, step, 0)

    def on_edges(body):
        each(0, 2, lambda side: body(side, side * (nx - 1), 2 + side * (nx - 3)))

    to_sides("q", lambda side: start.at[0, 0, edge(side)], halo(qe))
    to_sides("c", lambda side: cond.at[edge(side)], halo(c))
    for load in loads:
        load.wait()

    def first_edge(side, i, inner):
        e, r = qe[i + 1], qr[i]
        f = c[i + 1] * (qe[inner] + inplane(e)) + react(e, t[i]) - r
        g = k[i] * (e - 0.5 * r)
        f0e[i], f0r[i] = f, g
        n1 = e + 0.5 * f
        n1e[i + 1], n1s[side], n1r[i] = n1, n1, r + 0.5 * g

    on_edges(first_edge)
    to_sides("n1p", slot(n1s), slot(n1h))

    def slow_step(i):
        g = k[i] * (n1e[i + 1] - 0.5 * n1r[i])
        t1r[i] = g
        n2r[i] = n1r[i] + 0.5 * g

    def first_inner(i):
        e, r = qe[i + 1], qr[i]
        f = c[i + 1] * (qe[i] + qe[i + 2] + inplane(e)) + react(e, t[i]) - r
        g = k[i] * (e - 0.5 * r)
        f0e[i], f0r[i] = f, g
        n1e[i + 1], n1r[i] = e + 0.5 * f, r + 0.5 * g
        slow_step(i)

    each(1, nx - 1, first_inner)

    def hand_over(kind, part, ref, shift, dst, low, count):
        src = ref.at[pl.ds(low + shift, count)]
        send((kind, part), src, dst.at[pl.ds(low, count)], later, 1)

    hand_over("n2r", 2, n2r, 0, rn2r, 1, nx - 2)

    def second(i):
        e = n1e[i + 1]
        f = c[i + 1] * (n1e[i] + n1e[i + 2] + inplane(e)) + react(e, t[i]) - n1r[i]
        t1e[i] = f
        n2e[i + 1] = e + 0.5 * f

    each(2, nx - 2, second)
    hand_over("n2e", 2, n2e, 1, rn2e, 2, nx - 4)

    def coarse_coeffs(j):
        for fine, shift, coarse in ((c, 1, cc), (t, 0, tc), (k, 0, kc)):
            coarse[j] = 0.25 * pair(fine[2 * j + shift] + fine[2 * j + 1 + shift])

    each(0, cn, coarse_coeffs)

    for side in (0, 1):
        i, end = edge(side), side * (nx + 1)
        from_side("q", side, qe.at[end])
        from_side("c", side, c.at[end])
        from_side("n1p", side, n1h.at[side])
        more = c[i + 1] * qe[end]
        f0e[i] += more
        n1e[i + 1] += 0.5 * more
        n1e[end] = n1h[side] + 0.5 * c[end] * qe[i + 1]
        slow_step(i)

    on_edges(lambda side, i, inner: second(i))
    own_edge = lambda ref: lambda side: ref.at[edge(side) + 1]
    to_sides("n2", own_edge(n2e), halo(n2e))
    on_edges(lambda side, i, inner: second(inner - 1))
    for side in (0, 1):
        hand_over("n2e", side, n2e, 1, rn2e, side * (nx - 2), 2)
        hand_over("n2r", side, n2r, 0, rn2r, edge(side), 1)

    def third(j, e_ref, r_ref, extra, missing=None):
        sums = [0.0, 0.0, 0.0, 0.0]
        for row in (0, 1):
            i = 2 * j + row
            e, r = e_ref[i + 1], r_ref[i]
            if missing == 0 and row == 0:
                x = e_ref[i + 2]
            elif missing == 1 and row == 1:
                x = e_ref[i]
            else:
                x = e_ref[i] + e_ref[i + 2]
            fe = c[i + 1] * (x + inplane(e)) + react(e, t[i]) - r
            fr = k[i] * (e - 0.5 * r)
            a, b, g, h = extra(i)
            sums[0] += a - W24 * fe
            sums[1] += b - W24 * fr
            sums[2] += g + SIXTH * fe
            sums[3] += h + SIXTH * fr
        dE[j + 1] = 0.25 * pair(sums[0])
        dR[j] = 0.25 * pair(sums[1])
        jE[j] = 0.25 * pair(sums[2])
        jR[j] = 0.25 * pair(sums[3])

    def extra_first(i):
        a, b, g, h = f0e[i], t1e[i], f0r[i], t1r[i]
        return (
            8 * W24 * b - 7 * W24 * a,
            8 * W24 * h - 7 * W24 * g,
            SIXTH * b - 2 * SIXTH * a,
            SIXTH * h - 2 * SIXTH * g,
        )

    for side in (0, 1):
        third(side * (cn - 1), n2e, n2r, extra_first, side)
        ds[side] = fold(dE[side * (cn - 1) + 1])
    to_sides("dp", slot(ds), slot(dh))
    to_later_sides("n2x", own_edge(n2e), slot(n2xh))
    each(1, cn - 1, lambda j: third(j, n2e, n2r, extra_first))

    for side in (0, 1):
        i, j, end = edge(side), side * (cn - 1), side * (nx + 1)
        from_side("n2", side, n2e.at[end])
        from_side("dp", side, dh.at[side])
        more = 0.25 * pair(c[i + 1] * n2e[end])
        dE[j + 1] -= W24 * more
        jE[j] += SIXTH * more
        dE[side * (cn + 1)] = unfold(dh[side]) - (0.25 * W24) * pair(c[end] * n2e[i + 1])

    def coarse_step(j, node, x):
        d, dr = dE[j + 1], dR[j]
        lap = 0.25 * (x + near(d, 0, 2)) + near(d, 1, 1) - 3.0 * d
        b = 0.25 * pair(node[2 * j + 1] + node[2 * j + 2])
        return 0.5 * (cc[j] * lap + react(b + d, tc[j]) - react(b, tc[j]) - dr)

    def coarse_slow(j):
        return jR[j] + 0.5 * kc[j] * (dE[j + 1] - 0.5 * dR[j])

    def coarse_first(j):
        e = jE[j] + coarse_step(j, n1e, dE[j] + dE[j + 2])
        r = coarse_slow(j)
        jE[j], jR[j] = e, r
        jts[j] = jnp.where(even_rows(e), e, r)

    each(0, 2, lambda side: coarse_first(side * (cn - 1)))
    for side in (0, 1):
        js[side] = fold(jE[side * (cn - 1)])
    to_sides("j", slot(js), slot(jh))
    to_later_sides("jx", slot(js), slot(jxh))
    each(1, cn - 1, coarse_first)
    send("jt", jts, jth, later, 1)

    def correct(j):
        for row in (0, 1):
            i = 2 * j + row
            u1e[i + 1] = n1e[i + 1] + dE[j + 1]
            u2e[i + 1] = n2e[i + 1] + jE[j]

    each(0, cn, correct)
    for side in (0, 1):
        end = side * (nx + 1)
        u1e[end] = n1e[end] + dE[side * (cn + 1)]
        u2e[end] = zeros

    def old_terms(j):
        for row in (0, 1):
            i = 2 * j + row
            u1, u2 = u1e[i + 1], u2e[i + 1]
            u1r, u2r = n1r[i] + dR[j], n2r[i] + jR[j]
            a1 = c[i + 1] * (u1e[i] + u1e[i + 2] + inplane(u1)) + react(u1, t[i]) - u1r
            a2 = c[i + 1] * (u2e[i] + u2e[i + 2] + inplane(u2)) + react(u2, t[i]) - u2r
            b1 = k[i] * (u1 - 0.5 * u1r)
            b2 = k[i] * (u2 - 0.5 * u2r)
            a0, b0 = f0e[i], f0r[i]
            s1e[i] = 8 * W24 * a1 - 7 * W24 * a0 - W24 * a2
            s1r[i] = 8 * W24 * b1 - 7 * W24 * b0 - W24 * b2
            s2e[i] = 5 * W24 * a2 - W24 * a0 - 4 * W24 * a1
            s2r[i] = 5 * W24 * b2 - W24 * b0 - 4 * W24 * b1

    each(0, cn, old_terms)

    for side in (0, 1):
        i, end = edge(side), side * (nx + 1)
        from_side("j", side, jh.at[side])
        more = c[i + 1] * (n2e[end] + unfold(jh[side]))
        s1e[i] -= W24 * more
        s2e[i] += 5 * W24 * more

    receive(("n2r", 2), rn2r.at[pl.ds(1, nx - 2)], earlier)
    receive(("n2e", 2), rn2e.at[pl.ds(2, nx - 4)], earlier)
    for side in (0, 1):
        receive(("n2r", side), rn2r.at[pl.ds(edge(side), 1)], earlier)
        receive(("n2e", side), rn2e.at[pl.ds(side * (nx - 2), 2)], earlier)
    for side in (0, 1):
        from_side("n2x", side, n2xh.at[side], earlier)
        from_side("jx", side, jxh.at[side], earlier)
        end = side * (nx + 1)
        qne[end] = jnp.where(head, qe[end], n2xh[side] + unfold(jxh[side]))
    receive("jt", jth, earlier)

    def arrive(j):
        e, r = expand(jth[j])
        for row in (0, 1):
            i = 2 * j + row
            qne[i + 1] = jnp.where(head, qe[i + 1], rn2e[i] + e)
            qnr[i] = jnp.where(head, qr[i], rn2r[i] + r)

    each(0, cn, arrive)

    def next_first(i):
        e, r = qne[i + 1], qnr[i]
        f = c[i + 1] * (qne[i] + qne[i + 2] + inplane(e)) + react(e, t[i]) - r
        g = k[i] * (e - 0.5 * r)
        t0e[i], t0r[i] = f, g
        m1e[i + 1] = e + 0.5 * f + s1e[i]
        m1r[i] = r + 0.5 * g + s1r[i]

    on_edges(lambda side, i, inner: next_first(i))
    to_sides("m1", own_edge(m1e), halo(m1e))
    on_edges(lambda side, i, inner: next_first(inner - 1))

    def next_second(i, x):
        e, r = m1e[i + 1], m1r[i]
        f = c[i + 1] * (x + inplane(e)) + react(e, t[i]) - r
        g = k[i] * (e - 0.5 * r)
        t1e[i], t1r[i] = f, g
        m2 = e + 0.5 * f + s2e[i]
        m2e[i + 1] = m2
        m2r[i] = r + 0.5 * g + s2r[i]
        return m2

    def next_edge(side, i, inner):
        m2s[side] = next_second(i, m1e[inner])

    on_edges(next_edge)
    to_sides("m2p", slot(m2s), slot(m2h))
    each(2, nx - 2, next_first)
    each(1, nx - 1, lambda i: next_second(i, m1e[i] + m1e[i + 2]))

    for side in (0, 1):
        i, end = edge(side), side * (nx + 1)
        from_side("m1", side, m1e.at[end])
        from_side("m2p", side, m2h.at[side])
        more = c[i + 1] * m1e[end]
        t1e[i] += more
        m2e[i + 1] += 0.5 * more
        m2e[end] = m2h[side] + 0.5 * c[end] * m1e[i + 1]

    def extra_next(i):
        a, b, g, h = t0e[i], t1e[i], t0r[i], t1r[i]
        return (
            8 * W24 * b - 7 * W24 * a - s1e[i],
            8 * W24 * h - 7 * W24 * g - s1r[i],
            SIXTH * b - 2 * SIXTH * a - s1e[i] - s2e[i],
            SIXTH * h - 2 * SIXTH * g - s1r[i] - s2r[i],
        )

    each(0, 2, lambda side: third(side * (cn - 1), m2e, m2r, extra_next))
    for side in (0, 1):
        d2s[side] = fold(dE[side * (cn - 1) + 1])
    to_sides("d2", slot(d2s), slot(d2h))
    each(1, cn - 1, lambda j: third(j, m2e, m2r, extra_next))

    def final_slow(j):
        r = coarse_slow(j)
        for row in (0, 1):
            orr[2 * j + row] = m2r[2 * j + row] + r

    each(0, cn, final_slow)
    stores = [pltpu.make_async_copy(orr, out.at[0, 1], store_sem.at[0])]
    stores[-1].start()

    def final_fast(j):
        e = jE[j] + coarse_step(j, m1e, dE[j] + dE[j + 2])
        for row in (0, 1):
            oe[2 * j + row] = m2e[2 * j + 1 + row] + e

    each(1, cn - 1, final_fast)
    if cn > 2:
        inside = pl.ds(2, nx - 4)
        stores.append(pltpu.make_async_copy(oe.at[inside], out.at[0, 0, inside], store_sem.at[1]))
        stores[-1].start()

    for side in (0, 1):
        j = side * (cn - 1)
        inner = dE[2 + side * (cn - 3)]
        e = jE[j] + coarse_step(j, m1e, inner)
        oe[2 * j] = m2e[2 * j + 1] + e
        oe[2 * j + 1] = m2e[2 * j + 2] + e
    for side in (0, 1):
        j = side * (cn - 1)
        from_side("d2", side, d2h.at[side])
        e = 0.125 * cc[j] * unfold(d2h[side])
        oe[2 * j] += e
        oe[2 * j + 1] += e
        rows = pl.ds(2 * j, 2)
        stores.append(
            pltpu.make_async_copy(oe.at[rows], out.at[0, 0, rows], store_sem.at[2 + side])
        )
        stores[-1].start()

    for name, src, dst, when, dp, dside in pending:

        @pl.when(when)
        def _():
            copy_of(name, src, dst, dp, dside).wait_send()

    for store in stores:
        store.wait()


def per_device(start, conduct, threshold, recovery):
    nx, ny, nz = conduct.shape
    cn = nx // 2

    def planes(count, rows=ny):
        return pltpu.VMEM((count, rows, nz), jnp.float32)

    own, padded, coarse, two, half = (
        planes(nx), planes(nx + 2), planes(cn), planes(2), planes(2, ny // 2)
    )
    scratch = [
        padded, own, padded, own, own, coarse, coarse, coarse,
        own, own, padded, own, padded, own, own, own,
        planes(cn + 2), coarse, coarse, coarse, padded, padded, own, own, own, own,
        padded, own, padded, own, padded, own, own, own, own, own,
        two, two, half, half, half, half, half, two, own, own, coarse, coarse,
        two, two, half, half,
        pltpu.SemaphoreType.DMA((5,)),
        pltpu.SemaphoreType.DMA((4,)),
        pltpu.SemaphoreType.DMA((len(MESSAGES),)),
        pltpu.SemaphoreType.DMA((len(MESSAGES),)),
    ]
    return pl.pallas_call(
        kernel,
        out_shape=jax.ShapeDtypeStruct(start.shape, jnp.float32),
        in_specs=[pl.BlockSpec(memory_space=pl.ANY)] * 4,
        out_specs=pl.BlockSpec(memory_space=pl.ANY),
        scratch_shapes=scratch,
        compiler_params=pltpu.CompilerParams(
            collective_id=0, has_side_effects=True, vmem_limit_bytes=62 * 1024 * 1024
        ),
    )(start, conduct, threshold, recovery)


def solution(mesh):
    placed = (
        P("tm", None, "space", None, None),
        P("space", None, None),
        P("space", None, None),
        P("space", None, None),
    )
    return jax.shard_map(
        per_device,
        mesh=mesh,
        in_specs=placed,
        out_specs=P("tm", None, "space", None, None),
        check_vma=False,
    )
```

```python
import functools
import jax
import jax.numpy as jnp
from jax import lax
from jax.experimental import pallas as pl
from jax.experimental.pallas import tpu as pltpu
from jax.sharding import PartitionSpec as P

MESH = pl.DeviceIdType.MESH
SIXTH = 1.0 / 6.0
W24 = 1.0 / 24.0


def react(e, t):
    return 2.0 * e * (1.0 - e) * (e - t)


def near(v, axis, by):
    if axis == 0:
        rows, lanes = v.shape
        groups = v.reshape(rows // 8, 8, lanes)
        at = lax.broadcasted_iota(jnp.int32, groups.shape, 1)
        none = jnp.zeros((1, 8, lanes), v.dtype)
        low = pltpu.roll(groups, by, 1)
        low = jnp.where(at < by, jnp.concatenate([none, low[:-1]], axis=0), low)
        high = pltpu.roll(groups, 8 - by, 1)
        high = jnp.where(at >= 8 - by, jnp.concatenate([high[1:], none], axis=0), high)
        return (low + high).reshape(rows, lanes)
    n = v.shape[axis]
    at = lax.broadcasted_iota(jnp.int32, v.shape, axis)
    low = jnp.where(at < by, 0.0, pltpu.roll(v, by, axis))
    high = jnp.where(at >= n - by, 0.0, pltpu.roll(v, n - by, axis))
    return low + high


def tiles(v, by):
    rows, lanes = v.shape
    return pltpu.roll(v.reshape(rows // 8, 8, lanes), by, 1).reshape(rows, lanes)


def even_rows(v):
    return lax.broadcasted_iota(jnp.int32, v.shape, 0) % 2 == 0


def pair(v):
    return v + jnp.where(even_rows(v), tiles(v, 7), tiles(v, 1))


def fold(v):
    half = v.shape[0] // 2
    return jnp.where(even_rows(v[:half]), v[:half], v[half:])


def expand(x):
    even = even_rows(x)
    return jnp.where(even, x, tiles(x, 1)), jnp.where(even, tiles(x, 7), x)


def unfold(x):
    return jnp.concatenate(expand(x), axis=0)


def inplane(e):
    return near(e, 0, 1) + near(e, 1, 1) - 6.0 * e


MESSAGES = {
    name: at
    for at, name in enumerate(
        [
            (kind, side)
            for kind in ("q", "c", "n1p", "n2", "dp", "n2x", "j", "jx", "m1", "m2p", "d2")
            for side in (0, 1)
        ]
        + [(kind, side) for kind in ("n2r", "n2e", "jt") for side in (0, 1, 2)]
    )
}


def kernel(
    start, cond, thr, rec, node_out, jump_out,
    qe, qr, c, t, k, cc, tc, kc,
    f0e, f0r, n1e, n1r, n2e, n2r, t1e, t1r,
    dE, dR, jE, jR, u1e, u2e, s1e, s1r, s2e, s2r,
    qne, qnr, m1e, m1r, m2e, m2r, t0e, t0r,
    n1s, n1h, ds, dh, js, jh, jxh, n2xh, rn2r, rn2e, jts, jth,
    m2s, m2h, d2s, d2h,
    load_sem, store_sem, send_sem, recv_sem,
):
    nx = qr.shape[0]
    cn = nx // 2
    p, s = lax.axis_index("tm"), lax.axis_index("space")
    slices, slabs = lax.axis_size("tm"), lax.axis_size("space")
    head = p == 0
    has = (s > 0, s < slabs - 1)
    earlier, later = p > 0, p < slices - 1
    plane = qe.shape[1:]
    zeros = jnp.zeros(plane, jnp.float32)

    loads = [
        pltpu.make_async_copy(src, dst, load_sem.at[i])
        for i, (src, dst) in enumerate(
            [
                (start.at[0, 0], qe.at[pl.ds(1, nx)]),
                (cond, c.at[pl.ds(1, nx)]),
                (thr, t),
                (start.at[0, 1], qr),
                (rec, k),
            ]
        )
    ]
    for load in loads:
        load.start()

    barrier = pltpu.get_barrier_semaphore()

    def greet(when, dp, dside):
        @pl.when(when)
        def _():
            pl.semaphore_signal(barrier, inc=1, device_id=(p + dp, s + dside), device_id_type=MESH)

    greet(has[0], 0, -1)
    greet(has[1], 0, 1)
    greet(earlier, -1, 0)
    greet(earlier & has[0], -1, -1)
    greet(earlier & has[1], -1, 1)

    for side in (0, 1):
        end = side * (nx + 1)

        @pl.when(jnp.logical_not(has[side]))
        def _():
            for ref in (qe, c):
                ref[end] = zeros
            for ref in (n1h, n2xh, m2h):
                ref[side] = zeros
            n2e[end] = zeros
            m1e[end] = zeros
            for ref in (dh, jh, jxh, d2h):
                ref[side] = zeros[: plane[0] // 2]

    sides = has[0].astype(jnp.int32) + has[1].astype(jnp.int32)
    after = later.astype(jnp.int32)
    pl.semaphore_wait(barrier, sides + after * (sides + 1))

    pending = []

    def copy_of(name, src, dst, dp, dside):
        at = MESSAGES[name]
        return pltpu.make_async_remote_copy(
            src_ref=src,
            dst_ref=dst,
            send_sem=send_sem.at[at],
            recv_sem=recv_sem.at[at],
            device_id=(p + dp, s + dside),
            device_id_type=MESH,
        )

    def send(name, src, dst, when, dp=0, dside=0):
        @pl.when(when)
        def _():
            copy_of(name, src, dst, dp, dside).start()

        pending.append((name, src, dst, when, dp, dside))

    def receive(name, dst, when):
        @pl.when(when)
        def _():
            copy_of(name, dst, dst, 0, 0).wait_recv()

    def to_sides(kind, src, dst):
        for side in (0, 1):
            send((kind, side), src(side), dst(1 - side), has[side], 0, 2 * side - 1)

    def to_later_sides(kind, src, dst):
        for side in (0, 1):
            send((kind, side), src(side), dst(1 - side), later & has[side], 1, 2 * side - 1)

    def from_side(kind, side, dst, when=None):
        receive((kind, 1 - side), dst, has[side] if when is None else when & has[side])

    def edge(side):
        return side * (nx - 1)

    def halo(ref):
        return lambda side: ref.at[side * (ref.shape[0] - 1)]

    def slot(ref):
        return lambda side: ref.at[side]

    def each(low, high, body):
        def step(i, _):
            body(i)
            return 0

        lax.fori_loop(low, high, step, 0)

    def on_edges(body):
        each(0, 2, lambda side: body(side, side * (nx - 1), 2 + side * (nx - 3)))

    to_sides("q", lambda side: start.at[0, 0, edge(side)], halo(qe))
    to_sides("c", lambda side: cond.at[edge(side)], halo(c))
    for load in loads:
        load.wait()

    def first_edge(side, i, inner):
        e, r = qe[i + 1], qr[i]
        f = c[i + 1] * (qe[inner] + inplane(e)) + react(e, t[i]) - r
        g = k[i] * (e - 0.5 * r)
        f0e[i], f0r[i] = f, g
        n1 = e + 0.5 * f
        n1e[i + 1], n1s[side], n1r[i] = n1, n1, r + 0.5 * g

    on_edges(first_edge)
    to_sides("n1p", slot(n1s), slot(n1h))

    def slow_step(i):
        g = k[i] * (n1e[i + 1] - 0.5 * n1r[i])
        t1r[i] = g
        n2r[i] = n1r[i] + 0.5 * g

    def first_inner(i):
        e, r = qe[i + 1], qr[i]
        f = c[i + 1] * (qe[i] + qe[i + 2] + inplane(e)) + react(e, t[i]) - r
        g = k[i] * (e - 0.5 * r)
        f0e[i], f0r[i] = f, g
        n1e[i + 1], n1r[i] = e + 0.5 * f, r + 0.5 * g
        slow_step(i)

    each(1, nx - 1, first_inner)

    def hand_over(kind, part, ref, shift, dst, low, count):
        src = ref.at[pl.ds(low + shift, count)]
        send((kind, part), src, dst.at[pl.ds(low, count)], later, 1)

    hand_over("n2r", 2, n2r, 0, rn2r, 1, nx - 2)

    def second(i):
        e = n1e[i + 1]
        f = c[i + 1] * (n1e[i] + n1e[i + 2] + inplane(e)) + react(e, t[i]) - n1r[i]
        t1e[i] = f
        n2e[i + 1] = e + 0.5 * f

    each(2, nx - 2, second)
    hand_over("n2e", 2, n2e, 1, rn2e, 2, nx - 4)

    def coarse_coeffs(j):
        for fine, shift, coarse in ((c, 1, cc), (t, 0, tc), (k, 0, kc)):
            coarse[j] = 0.25 * pair(fine[2 * j + shift] + fine[2 * j + 1 + shift])

    each(0, cn, coarse_coeffs)

    for side in (0, 1):
        i, end = edge(side), side * (nx + 1)
        from_side("q", side, qe.at[end])
        from_side("c", side, c.at[end])
        from_side("n1p", side, n1h.at[side])
        more = c[i + 1] * qe[end]
        f0e[i] += more
        n1e[i + 1] += 0.5 * more
        n1e[end] = n1h[side] + 0.5 * c[end] * qe[i + 1]
        slow_step(i)

    on_edges(lambda side, i, inner: second(i))
    own_edge = lambda ref: lambda side: ref.at[edge(side) + 1]
    to_sides("n2", own_edge(n2e), halo(n2e))
    on_edges(lambda side, i, inner: second(inner - 1))
    for side in (0, 1):
        hand_over("n2e", side, n2e, 1, rn2e, side * (nx - 2), 2)
        hand_over("n2r", side, n2r, 0, rn2r, edge(side), 1)

    def third(j, e_ref, r_ref, extra, missing=None):
        sums = [0.0, 0.0, 0.0, 0.0]
        for row in (0, 1):
            i = 2 * j + row
            e, r = e_ref[i + 1], r_ref[i]
            if missing == 0 and row == 0:
                x = e_ref[i + 2]
            elif missing == 1 and row == 1:
                x = e_ref[i]
            else:
                x = e_ref[i] + e_ref[i + 2]
            fe = c[i + 1] * (x + inplane(e)) + react(e, t[i]) - r
            fr = k[i] * (e - 0.5 * r)
            a, b, g, h = extra(i)
            sums[0] += a - W24 * fe
            sums[1] += b - W24 * fr
            sums[2] += g + SIXTH * fe
            sums[3] += h + SIXTH * fr
        dE[j + 1] = 0.25 * pair(sums[0])
        dR[j] = 0.25 * pair(sums[1])
        jE[j] = 0.25 * pair(sums[2])
        jR[j] = 0.25 * pair(sums[3])

    def extra_first(i):
        a, b, g, h = f0e[i], t1e[i], f0r[i], t1r[i]
        return (
            8 * W24 * b - 7 * W24 * a,
            8 * W24 * h - 7 * W24 * g,
            SIXTH * b - 2 * SIXTH * a,
            SIXTH * h - 2 * SIXTH * g,
        )

    for side in (0, 1):
        third(side * (cn - 1), n2e, n2r, extra_first, side)
        ds[side] = fold(dE[side * (cn - 1) + 1])
    to_sides("dp", slot(ds), slot(dh))
    to_later_sides("n2x", own_edge(n2e), slot(n2xh))
    each(1, cn - 1, lambda j: third(j, n2e, n2r, extra_first))

    def coarse_step(j, node, x):
        d, dr = dE[j + 1], dR[j]
        lap = 0.25 * (x + near(d, 0, 2)) + near(d, 1, 1) - 3.0 * d
        b = 0.25 * pair(node[2 * j + 1] + node[2 * j + 2])
        return 0.5 * (cc[j] * lap + react(b + d, tc[j]) - react(b, tc[j]) - dr)

    def coarse_slow(j):
        return jR[j] + 0.5 * kc[j] * (dE[j + 1] - 0.5 * dR[j])

    def coarse_first(j):
        e = jE[j] + coarse_step(j, n1e, dE[j] + dE[j + 2])
        r = coarse_slow(j)
        jE[j], jR[j] = e, r
        jts[j] = jnp.where(even_rows(e), e, r)

    each(1, cn - 1, coarse_first)
    send(("jt", 2), jts.at[pl.ds(1, cn - 2)], jth.at[pl.ds(1, cn - 2)], later, 1)

    for side in (0, 1):
        i, j, end = edge(side), side * (cn - 1), side * (nx + 1)
        from_side("n2", side, n2e.at[end])
        from_side("dp", side, dh.at[side])
        more = 0.25 * pair(c[i + 1] * n2e[end])
        change = W24 * more
        dE[j + 1] -= change
        beside = 1 + side * (cn - 3)
        jE[beside] -= 0.125 * cc[beside] * change
        jE[j] += SIXTH * more
        dE[side * (cn + 1)] = unfold(dh[side]) - (0.25 * W24) * pair(c[end] * n2e[i + 1])

    each(0, 2, lambda side: coarse_first(side * (cn - 1)))
    for side in (0, 1):
        js[side] = fold(jE[side * (cn - 1)])
    to_sides("j", slot(js), slot(jh))
    to_later_sides("jx", slot(js), slot(jxh))
    for side in (0, 1):
        last = pl.ds(side * (cn - 1), 1)
        send(("jt", side), jts.at[last], jth.at[last], later, 1)

    def correct(j):
        for row in (0, 1):
            i = 2 * j + row
            u1e[i + 1] = n1e[i + 1] + dE[j + 1]
            u2e[i + 1] = n2e[i + 1] + jE[j]

    each(0, cn, correct)
    for side in (0, 1):
        end = side * (nx + 1)
        u1e[end] = n1e[end] + dE[side * (cn + 1)]
        u2e[end] = zeros

    def old_terms(j):
        for row in (0, 1):
            i = 2 * j + row
            u1, u2 = u1e[i + 1], u2e[i + 1]
            u1r, u2r = n1r[i] + dR[j], n2r[i] + jR[j]
            a1 = c[i + 1] * (u1e[i] + u1e[i + 2] + inplane(u1)) + react(u1, t[i]) - u1r
            a2 = c[i + 1] * (u2e[i] + u2e[i + 2] + inplane(u2)) + react(u2, t[i]) - u2r
            b1 = k[i] * (u1 - 0.5 * u1r)
            b2 = k[i] * (u2 - 0.5 * u2r)
            a0, b0 = f0e[i], f0r[i]
            s1e[i] = 8 * W24 * a1 - 7 * W24 * a0 - W24 * a2
            s1r[i] = 8 * W24 * b1 - 7 * W24 * b0 - W24 * b2
            s2e[i] = 5 * W24 * a2 - W24 * a0 - 4 * W24 * a1
            s2r[i] = 5 * W24 * b2 - W24 * b0 - 4 * W24 * b1

    each(0, cn, old_terms)

    for side in (0, 1):
        i, end = edge(side), side * (nx + 1)
        from_side("j", side, jh.at[side])
        more = c[i + 1] * (n2e[end] + unfold(jh[side]))
        s1e[i] -= W24 * more
        s2e[i] += 5 * W24 * more

    receive(("n2r", 2), rn2r.at[pl.ds(1, nx - 2)], earlier)
    receive(("n2e", 2), rn2e.at[pl.ds(2, nx - 4)], earlier)
    for side in (0, 1):
        receive(("n2r", side), rn2r.at[pl.ds(edge(side), 1)], earlier)
        receive(("n2e", side), rn2e.at[pl.ds(side * (nx - 2), 2)], earlier)
    for side in (0, 1):
        from_side("n2x", side, n2xh.at[side], earlier)
        from_side("jx", side, jxh.at[side], earlier)
        end = side * (nx + 1)
        qne[end] = jnp.where(head, qe[end], n2xh[side] + unfold(jxh[side]))
    receive(("jt", 2), jth.at[pl.ds(1, cn - 2)], earlier)
    for side in (0, 1):
        receive(("jt", side), jth.at[pl.ds(side * (cn - 1), 1)], earlier)

    def arrive(j, side=None):
        e, r = expand(jth[j])
        if side is not None:
            e -= (0.125 * W24 * 0.25) * cc[j] * pair(c[edge(side) + 1] * n2xh[side])
        for row in (0, 1):
            i = 2 * j + row
            qne[i + 1] = jnp.where(head, qe[i + 1], rn2e[i] + e)
            qnr[i] = jnp.where(head, qr[i], rn2r[i] + r)

    each(0, 2, lambda side: arrive(side * (cn - 1)))
    for side in (0, 1):
        arrive(1 + side * (cn - 3), side)
    each(2, cn - 2, arrive)

    def next_first(i):
        e, r = qne[i + 1], qnr[i]
        f = c[i + 1] * (qne[i] + qne[i + 2] + inplane(e)) + react(e, t[i]) - r
        g = k[i] * (e - 0.5 * r)
        t0e[i], t0r[i] = f, g
        m1e[i + 1] = e + 0.5 * f + s1e[i]
        m1r[i] = r + 0.5 * g + s1r[i]

    on_edges(lambda side, i, inner: next_first(i))
    to_sides("m1", own_edge(m1e), halo(m1e))
    on_edges(lambda side, i, inner: next_first(inner - 1))

    def next_second(i, x):
        e, r = m1e[i + 1], m1r[i]
        f = c[i + 1] * (x + inplane(e)) + react(e, t[i]) - r
        g = k[i] * (e - 0.5 * r)
        t1e[i], t1r[i] = f, g
        m2 = e + 0.5 * f + s2e[i]
        m2e[i + 1] = m2
        m2r[i] = r + 0.5 * g + s2r[i]
        return m2

    def next_edge(side, i, inner):
        m2s[side] = next_second(i, m1e[inner])

    on_edges(next_edge)
    to_sides("m2p", slot(m2s), slot(m2h))
    each(2, nx - 2, next_first)
    each(1, nx - 1, lambda i: next_second(i, m1e[i] + m1e[i + 2]))

    for side in (0, 1):
        i, end = edge(side), side * (nx + 1)
        from_side("m1", side, m1e.at[end])
        from_side("m2p", side, m2h.at[side])
        more = c[i + 1] * m1e[end]
        t1e[i] += more
        m2e[i + 1] += 0.5 * more
        m2e[end] = m2h[side] + 0.5 * c[end] * m1e[i + 1]

    stores = []

    def store(src, dst):
        stores.append(pltpu.make_async_copy(src, dst, store_sem.at[len(stores)]))
        stores[-1].start()

    store(m2e.at[pl.ds(1, nx)], node_out.at[0])
    store(m2r, node_out.at[1])

    def extra_next(i):
        a, b, g, h = t0e[i], t1e[i], t0r[i], t1r[i]
        return (
            8 * W24 * b - 7 * W24 * a - s1e[i],
            8 * W24 * h - 7 * W24 * g - s1r[i],
            SIXTH * b - 2 * SIXTH * a - s1e[i] - s2e[i],
            SIXTH * h - 2 * SIXTH * g - s1r[i] - s2r[i],
        )

    each(0, 2, lambda side: third(side * (cn - 1), m2e, m2r, extra_next))
    for side in (0, 1):
        d2s[side] = fold(dE[side * (cn - 1) + 1])
    to_sides("d2", slot(d2s), slot(d2h))
    each(1, cn - 1, lambda j: third(j, m2e, m2r, extra_next))

    def final_slow(j):
        jR[j] = coarse_slow(j)

    each(0, cn, final_slow)
    store(jR, jump_out.at[1])

    def final_fast(j):
        jE[j] += coarse_step(j, m1e, dE[j] + dE[j + 2])

    each(1, cn - 1, final_fast)
    inside = pl.ds(1, cn - 2)
    store(jE.at[inside], jump_out.at[0, inside])

    for side in (0, 1):
        j = side * (cn - 1)
        jE[j] += coarse_step(j, m1e, dE[2 + side * (cn - 3)])
    for side in (0, 1):
        j = side * (cn - 1)
        from_side("d2", side, d2h.at[side])
        jE[j] += 0.125 * cc[j] * unfold(d2h[side])
        store(jE.at[j], jump_out.at[0, j])

    for name, src, dst, when, dp, dside in pending:

        @pl.when(when)
        def _():
            copy_of(name, src, dst, dp, dside).wait_send()

    for stored in stores:
        stored.wait()


def per_device(start, conduct, threshold, recovery):
    nx, ny, nz = conduct.shape
    cn = nx // 2

    def planes(count, rows=ny):
        return pltpu.VMEM((count, rows, nz), jnp.float32)

    own, padded, coarse, two, half = (
        planes(nx), planes(nx + 2), planes(cn), planes(2), planes(2, ny // 2)
    )
    scratch = [
        padded, own, padded, own, own, coarse, coarse, coarse,
        own, own, padded, own, padded, own, own, own,
        planes(cn + 2), coarse, coarse, coarse, padded, padded, own, own, own, own,
        padded, own, padded, own, padded, own, own, own,
        two, two, half, half, half, half, half, two, own, own, coarse, coarse,
        two, two, half, half,
        pltpu.SemaphoreType.DMA((5,)),
        pltpu.SemaphoreType.DMA((6,)),
        pltpu.SemaphoreType.DMA((len(MESSAGES),)),
        pltpu.SemaphoreType.DMA((len(MESSAGES),)),
    ]
    nodes, jumps = pl.pallas_call(
        kernel,
        out_shape=[
            jax.ShapeDtypeStruct((2, nx, ny, nz), jnp.float32),
            jax.ShapeDtypeStruct((2, cn, ny, nz), jnp.float32),
        ],
        in_specs=[pl.BlockSpec(memory_space=pl.ANY)] * 4,
        out_specs=[pl.BlockSpec(memory_space=pl.ANY)] * 2,
        scratch_shapes=scratch,
        compiler_params=pltpu.CompilerParams(
            collective_id=0, has_side_effects=True, vmem_limit_bytes=62 * 1024 * 1024
        ),
    )(start, conduct, threshold, recovery)
    corrected = nodes.reshape(2, cn, 2, ny, nz) + jumps[:, :, None]
    return corrected.reshape(start.shape)


def solution(mesh):
    placed = (
        P("tm", None, "space", None, None),
        P("space", None, None),
        P("space", None, None),
        P("space", None, None),
    )
    return jax.shard_map(
        per_device,
        mesh=mesh,
        in_specs=placed,
        out_specs=P("tm", None, "space", None, None),
        check_vma=False,
    )
```

```python
import functools
import jax
import jax.numpy as jnp
from jax import lax
from jax.experimental import pallas as pl
from jax.experimental.pallas import tpu as pltpu
from jax.sharding import PartitionSpec as P

MESH = pl.DeviceIdType.MESH
SIXTH = 1.0 / 6.0
W24 = 1.0 / 24.0


def react(e, t):
    return 2.0 * e * (1.0 - e) * (e - t)


def near(v, axis, by):
    if axis == 0:
        rows, lanes = v.shape
        groups = v.reshape(rows // 8, 8, lanes)
        at = lax.broadcasted_iota(jnp.int32, groups.shape, 1)
        none = jnp.zeros((1, 8, lanes), v.dtype)
        low = pltpu.roll(groups, by, 1)
        low = jnp.where(at < by, jnp.concatenate([none, low[:-1]], axis=0), low)
        high = pltpu.roll(groups, 8 - by, 1)
        high = jnp.where(at >= 8 - by, jnp.concatenate([high[1:], none], axis=0), high)
        return (low + high).reshape(rows, lanes)
    n = v.shape[axis]
    at = lax.broadcasted_iota(jnp.int32, v.shape, axis)
    low = jnp.where(at < by, 0.0, pltpu.roll(v, by, axis))
    high = jnp.where(at >= n - by, 0.0, pltpu.roll(v, n - by, axis))
    return low + high


def tiles(v, by):
    rows, lanes = v.shape
    return pltpu.roll(v.reshape(rows // 8, 8, lanes), by, 1).reshape(rows, lanes)


def even_rows(v):
    return lax.broadcasted_iota(jnp.int32, v.shape, 0) % 2 == 0


def pair(v):
    return v + jnp.where(even_rows(v), tiles(v, 7), tiles(v, 1))


def fold(v):
    half = v.shape[0] // 2
    return jnp.where(even_rows(v[:half]), v[:half], v[half:])


def expand(x):
    even = even_rows(x)
    return jnp.where(even, x, tiles(x, 1)), jnp.where(even, tiles(x, 7), x)


def unfold(x):
    return jnp.concatenate(expand(x), axis=0)


def inplane(e):
    return near(e, 0, 1) + near(e, 1, 1) - 6.0 * e


MESSAGES = {
    name: at
    for at, name in enumerate(
        [
            (kind, side)
            for kind in ("q", "c", "n1p", "n2", "dp", "n2x", "j", "jx", "m1", "m2p", "dw", "t1", "c2")
            for side in (0, 1)
        ]
        + [(kind, side) for kind in ("n2r", "n2e", "jt") for side in (0, 1, 2)]
    )
}


def kernel(
    start, cond, thr, rec, node_out, jump_out,
    qe, qr, c, t, k, cc, tc, kc,
    f0e, f0r, n1e, n1r, n2e, n2r, t1e, t1r,
    dE, dR, jE, jR, u1e, u2e, s1e, s1r, s2e, s2r,
    qne, qnr, m1e, m1r, m2e, m2r, t0e, t0r,
    n1s, n1h, ds, dh, js, jh, jxh, n2xh, rn2r, rn2e, jts, jth,
    m2s, m2h, dws, dwh, t1h, c2h,
    load_sem, store_sem, send_sem, recv_sem,
):
    nx = qr.shape[0]
    cn = nx // 2
    p, s = lax.axis_index("tm"), lax.axis_index("space")
    slices, slabs = lax.axis_size("tm"), lax.axis_size("space")
    head = p == 0
    has = (s > 0, s < slabs - 1)
    earlier, later = p > 0, p < slices - 1
    plane = qe.shape[1:]
    zeros = jnp.zeros(plane, jnp.float32)

    loads = [
        pltpu.make_async_copy(src, dst, load_sem.at[i])
        for i, (src, dst) in enumerate(
            [
                (start.at[0, 0], qe.at[pl.ds(1, nx)]),
                (cond, c.at[pl.ds(1, nx)]),
                (thr, t),
                (start.at[0, 1], qr),
                (rec, k),
            ]
        )
    ]
    for load in loads:
        load.start()

    barrier = pltpu.get_barrier_semaphore()

    def greet(when, dp, dside):
        @pl.when(when)
        def _():
            pl.semaphore_signal(barrier, inc=1, device_id=(p + dp, s + dside), device_id_type=MESH)

    greet(has[0], 0, -1)
    greet(has[1], 0, 1)
    greet(earlier, -1, 0)
    greet(earlier & has[0], -1, -1)
    greet(earlier & has[1], -1, 1)

    for side in (0, 1):
        end = side * (nx + 1)

        @pl.when(jnp.logical_not(has[side]))
        def _():
            for ref in (qe, c):
                ref[end] = zeros
            for ref in (n1h, n2xh, m2h, t1h, c2h):
                ref[side] = zeros
            n2e[end] = zeros
            m1e[end] = zeros
            for ref in (dh, jh, jxh, dwh):
                ref[side] = zeros[: plane[0] // 2]

    sides = has[0].astype(jnp.int32) + has[1].astype(jnp.int32)
    after = later.astype(jnp.int32)
    pl.semaphore_wait(barrier, sides + after * (sides + 1))

    pending = []

    def copy_of(name, src, dst, dp, dside):
        at = MESSAGES[name]
        return pltpu.make_async_remote_copy(
            src_ref=src,
            dst_ref=dst,
            send_sem=send_sem.at[at],
            recv_sem=recv_sem.at[at],
            device_id=(p + dp, s + dside),
            device_id_type=MESH,
        )

    def send(name, src, dst, when, dp=0, dside=0):
        @pl.when(when)
        def _():
            copy_of(name, src, dst, dp, dside).start()

        pending.append((name, src, dst, when, dp, dside))

    def receive(name, dst, when):
        @pl.when(when)
        def _():
            copy_of(name, dst, dst, 0, 0).wait_recv()

    def to_sides(kind, src, dst):
        for side in (0, 1):
            send((kind, side), src(side), dst(1 - side), has[side], 0, 2 * side - 1)

    def to_later_sides(kind, src, dst):
        for side in (0, 1):
            send((kind, side), src(side), dst(1 - side), later & has[side], 1, 2 * side - 1)

    def from_side(kind, side, dst, when=None):
        receive((kind, 1 - side), dst, has[side] if when is None else when & has[side])

    def edge(side):
        return side * (nx - 1)

    def halo(ref):
        return lambda side: ref.at[side * (ref.shape[0] - 1)]

    def slot(ref):
        return lambda side: ref.at[side]

    def each(low, high, body):
        def step(i, _):
            body(i)
            return 0

        lax.fori_loop(low, high, step, 0)

    def on_edges(body):
        each(0, 2, lambda side: body(side, side * (nx - 1), 2 + side * (nx - 3)))

    to_sides("q", lambda side: start.at[0, 0, edge(side)], halo(qe))
    to_sides("c", lambda side: cond.at[edge(side)], halo(c))
    for load in loads:
        load.wait()

    def first_edge(side, i, inner):
        e, r = qe[i + 1], qr[i]
        f = c[i + 1] * (qe[inner] + inplane(e)) + react(e, t[i]) - r
        g = k[i] * (e - 0.5 * r)
        f0e[i], f0r[i] = f, g
        n1 = e + 0.5 * f
        n1e[i + 1], n1s[side], n1r[i] = n1, n1, r + 0.5 * g

    on_edges(first_edge)
    to_sides("n1p", slot(n1s), slot(n1h))

    def slow_step(i):
        g = k[i] * (n1e[i + 1] - 0.5 * n1r[i])
        t1r[i] = g
        n2r[i] = n1r[i] + 0.5 * g

    def first_inner(i):
        e, r = qe[i + 1], qr[i]
        f = c[i + 1] * (qe[i] + qe[i + 2] + inplane(e)) + react(e, t[i]) - r
        g = k[i] * (e - 0.5 * r)
        f0e[i], f0r[i] = f, g
        n1e[i + 1], n1r[i] = e + 0.5 * f, r + 0.5 * g
        slow_step(i)

    each(1, nx - 1, first_inner)

    def hand_over(kind, part, ref, shift, dst, low, count):
        src = ref.at[pl.ds(low + shift, count)]
        send((kind, part), src, dst.at[pl.ds(low, count)], later, 1)

    hand_over("n2r", 2, n2r, 0, rn2r, 1, nx - 2)

    def second(i):
        e = n1e[i + 1]
        f = c[i + 1] * (n1e[i] + n1e[i + 2] + inplane(e)) + react(e, t[i]) - n1r[i]
        t1e[i] = f
        n2e[i + 1] = e + 0.5 * f

    each(2, nx - 2, second)
    hand_over("n2e", 2, n2e, 1, rn2e, 2, nx - 4)

    def coarse_coeffs(j):
        for fine, shift, coarse in ((c, 1, cc), (t, 0, tc), (k, 0, kc)):
            coarse[j] = 0.25 * pair(fine[2 * j + shift] + fine[2 * j + 1 + shift])

    each(0, cn, coarse_coeffs)

    for side in (0, 1):
        i, end = edge(side), side * (nx + 1)
        from_side("q", side, qe.at[end])
        from_side("c", side, c.at[end])
        from_side("n1p", side, n1h.at[side])
        more = c[i + 1] * qe[end]
        f0e[i] += more
        n1e[i + 1] += 0.5 * more
        n1e[end] = n1h[side] + 0.5 * c[end] * qe[i + 1]
        slow_step(i)

    on_edges(lambda side, i, inner: second(i))
    own_edge = lambda ref: lambda side: ref.at[edge(side) + 1]
    to_sides("n2", own_edge(n2e), halo(n2e))
    on_edges(lambda side, i, inner: second(inner - 1))
    for side in (0, 1):
        hand_over("n2e", side, n2e, 1, rn2e, side * (nx - 2), 2)
        hand_over("n2r", side, n2r, 0, rn2r, edge(side), 1)

    def third(j, e_ref, r_ref, extra, missing=None):
        sums = [0.0, 0.0, 0.0, 0.0]
        for row in (0, 1):
            i = 2 * j + row
            e, r = e_ref[i + 1], r_ref[i]
            if missing == 0 and row == 0:
                x = e_ref[i + 2]
            elif missing == 1 and row == 1:
                x = e_ref[i]
            else:
                x = e_ref[i] + e_ref[i + 2]
            fe = c[i + 1] * (x + inplane(e)) + react(e, t[i]) - r
            fr = k[i] * (e - 0.5 * r)
            a, b, g, h = extra(i)
            sums[0] += a - W24 * fe
            sums[1] += b - W24 * fr
            sums[2] += g + SIXTH * fe
            sums[3] += h + SIXTH * fr
        dE[j + 1] = 0.25 * pair(sums[0])
        dR[j] = 0.25 * pair(sums[1])
        jE[j] = 0.25 * pair(sums[2])
        jR[j] = 0.25 * pair(sums[3])

    def extra_first(i):
        a, b, g, h = f0e[i], t1e[i], f0r[i], t1r[i]
        return (
            8 * W24 * b - 7 * W24 * a,
            8 * W24 * h - 7 * W24 * g,
            SIXTH * b - 2 * SIXTH * a,
            SIXTH * h - 2 * SIXTH * g,
        )

    for side in (0, 1):
        third(side * (cn - 1), n2e, n2r, extra_first, side)
        ds[side] = fold(dE[side * (cn - 1) + 1])
    to_sides("dp", slot(ds), slot(dh))
    to_later_sides("n2x", own_edge(n2e), slot(n2xh))
    each(1, cn - 1, lambda j: third(j, n2e, n2r, extra_first))

    def coarse_step(j, node, x):
        d, dr = dE[j + 1], dR[j]
        lap = 0.25 * (x + near(d, 0, 2)) + near(d, 1, 1) - 3.0 * d
        b = 0.25 * pair(node[2 * j + 1] + node[2 * j + 2])
        return 0.5 * (cc[j] * lap + react(b + d, tc[j]) - react(b, tc[j]) - dr)

    def coarse_slow(j):
        return jR[j] + 0.5 * kc[j] * (dE[j + 1] - 0.5 * dR[j])

    def coarse_first(j):
        e = jE[j] + coarse_step(j, n1e, dE[j] + dE[j + 2])
        r = coarse_slow(j)
        jE[j], jR[j] = e, r
        jts[j] = jnp.where(even_rows(e), e, r)

    each(1, cn - 1, coarse_first)
    send(("jt", 2), jts.at[pl.ds(1, cn - 2)], jth.at[pl.ds(1, cn - 2)], later, 1)

    for side in (0, 1):
        i, j, end = edge(side), side * (cn - 1), side * (nx + 1)
        from_side("n2", side, n2e.at[end])
        from_side("dp", side, dh.at[side])
        more = 0.25 * pair(c[i + 1] * n2e[end])
        change = W24 * more
        dE[j + 1] -= change
        beside = 1 + side * (cn - 3)
        jE[beside] -= 0.125 * cc[beside] * change
        jE[j] += SIXTH * more
        dE[side * (cn + 1)] = unfold(dh[side]) - (0.25 * W24) * pair(c[end] * n2e[i + 1])

    each(0, 2, lambda side: coarse_first(side * (cn - 1)))
    for side in (0, 1):
        js[side] = fold(jE[side * (cn - 1)])
    to_sides("j", slot(js), slot(jh))
    to_later_sides("jx", slot(js), slot(jxh))
    for side in (0, 1):
        last = pl.ds(side * (cn - 1), 1)
        send(("jt", side), jts.at[last], jth.at[last], later, 1)

    to_sides("t1", lambda side: thr.at[edge(side)], slot(t1h))
    to_sides("c2", lambda side: cond.at[1 + side * (nx - 3)], slot(c2h))

    def correct(j):
        for row in (0, 1):
            i = 2 * j + row
            u1e[i + 1] = n1e[i + 1] + dE[j + 1]
            u2e[i + 1] = n2e[i + 1] + jE[j]

    each(0, cn, correct)
    for side in (0, 1):
        end = side * (nx + 1)
        u1e[end] = n1e[end] + dE[side * (cn + 1)]
        u2e[end] = zeros

    def old_terms(j):
        for row in (0, 1):
            i = 2 * j + row
            u1, u2 = u1e[i + 1], u2e[i + 1]
            u1r, u2r = n1r[i] + dR[j], n2r[i] + jR[j]
            a1 = c[i + 1] * (u1e[i] + u1e[i + 2] + inplane(u1)) + react(u1, t[i]) - u1r
            a2 = c[i + 1] * (u2e[i] + u2e[i + 2] + inplane(u2)) + react(u2, t[i]) - u2r
            b1 = k[i] * (u1 - 0.5 * u1r)
            b2 = k[i] * (u2 - 0.5 * u2r)
            a0, b0 = f0e[i], f0r[i]
            s1e[i] = 8 * W24 * a1 - 7 * W24 * a0 - W24 * a2
            s1r[i] = 8 * W24 * b1 - 7 * W24 * b0 - W24 * b2
            s2e[i] = 5 * W24 * a2 - W24 * a0 - 4 * W24 * a1
            s2r[i] = 5 * W24 * b2 - W24 * b0 - 4 * W24 * b1

    each(0, cn, old_terms)

    for side in (0, 1):
        i, end = edge(side), side * (nx + 1)
        from_side("j", side, jh.at[side])
        more = c[i + 1] * (n2e[end] + unfold(jh[side]))
        s1e[i] -= W24 * more
        s2e[i] += 5 * W24 * more

    receive(("n2r", 2), rn2r.at[pl.ds(1, nx - 2)], earlier)
    receive(("n2e", 2), rn2e.at[pl.ds(2, nx - 4)], earlier)
    for side in (0, 1):
        receive(("n2r", side), rn2r.at[pl.ds(edge(side), 1)], earlier)
        receive(("n2e", side), rn2e.at[pl.ds(side * (nx - 2), 2)], earlier)
    for side in (0, 1):
        from_side("n2x", side, n2xh.at[side], earlier)
        from_side("jx", side, jxh.at[side], earlier)
        end = side * (nx + 1)
        qne[end] = jnp.where(head, qe[end], n2xh[side] + unfold(jxh[side]))
    receive(("jt", 2), jth.at[pl.ds(1, cn - 2)], earlier)
    for side in (0, 1):
        receive(("jt", side), jth.at[pl.ds(side * (cn - 1), 1)], earlier)

    def arrive(j, side=None):
        e, r = expand(jth[j])
        if side is not None:
            e -= (0.125 * W24 * 0.25) * cc[j] * pair(c[edge(side) + 1] * n2xh[side])
        for row in (0, 1):
            i = 2 * j + row
            qne[i + 1] = jnp.where(head, qe[i + 1], rn2e[i] + e)
            qnr[i] = jnp.where(head, qr[i], rn2r[i] + r)

    each(0, 2, lambda side: arrive(side * (cn - 1)))
    for side in (0, 1):
        arrive(1 + side * (cn - 3), side)
    each(2, cn - 2, arrive)

    def next_first(i):
        e, r = qne[i + 1], qnr[i]
        f = c[i + 1] * (qne[i] + qne[i + 2] + inplane(e)) + react(e, t[i]) - r
        g = k[i] * (e - 0.5 * r)
        t0e[i], t0r[i] = f, g
        m1e[i + 1] = e + 0.5 * f + s1e[i]
        m1r[i] = r + 0.5 * g + s1r[i]

    on_edges(lambda side, i, inner: next_first(i))
    to_sides("m1", own_edge(m1e), halo(m1e))
    on_edges(lambda side, i, inner: next_first(inner - 1))

    def next_second(i, x):
        e, r = m1e[i + 1], m1r[i]
        f = c[i + 1] * (x + inplane(e)) + react(e, t[i]) - r
        g = k[i] * (e - 0.5 * r)
        t1e[i], t1r[i] = f, g
        m2 = e + 0.5 * f + s2e[i]
        m2e[i + 1] = m2
        m2r[i] = r + 0.5 * g + s2r[i]
        return m2

    def next_edge(side, i, inner):
        m2s[side] = next_second(i, m1e[inner])

    on_edges(next_edge)
    to_sides("m2p", slot(m2s), slot(m2h))
    each(2, nx - 2, next_first)
    each(1, nx - 1, lambda i: next_second(i, m1e[i] + m1e[i + 2]))

    def defect(i):
        return 8 * W24 * t1e[i] - 7 * W24 * t0e[i] - s1e[i]

    def next_defect(side, i, inner):
        second, third_at = inner - 1, 2 + side * (nx - 5)
        e = m2e[second + 1]
        rest = c[second + 1] * (m2e[third_at + 1] + inplane(e)) + react(e, t[second])
        rest = rest - m2r[second] - m2r[i] + c[i + 1] * e
        dws[side] = fold(0.25 * pair(defect(i) + defect(second) - W24 * rest))

    on_edges(next_defect)
    to_sides("dw", slot(dws), slot(dwh))

    for side in (0, 1):
        i, end = edge(side), side * (nx + 1)
        from_side("m1", side, m1e.at[end])
        from_side("m2p", side, m2h.at[side])
        more = c[i + 1] * m1e[end]
        t1e[i] += more
        m2e[i + 1] += 0.5 * more
        m2e[end] = m2h[side] + 0.5 * c[end] * m1e[i + 1]

    stores = []

    def store(src, dst):
        stores.append(pltpu.make_async_copy(src, dst, store_sem.at[len(stores)]))
        stores[-1].start()

    store(m2e.at[pl.ds(1, nx)], node_out.at[0])
    store(m2r, node_out.at[1])

    def extra_next(i):
        a, b, g, h = t0e[i], t1e[i], t0r[i], t1r[i]
        return (
            8 * W24 * b - 7 * W24 * a - s1e[i],
            8 * W24 * h - 7 * W24 * g - s1r[i],
            SIXTH * b - 2 * SIXTH * a - s1e[i] - s2e[i],
            SIXTH * h - 2 * SIXTH * g - s1r[i] - s2r[i],
        )

    each(0, cn, lambda j: third(j, m2e, m2r, extra_next))

    def final_slow(j):
        jR[j] = coarse_slow(j)

    each(0, cn, final_slow)
    for row in (0, 1):
        store(jR, jump_out.at[1, :, row])

    for side in (0, 1):
        i, end = edge(side), side * (nx + 1)
        from_side("dw", side, dwh.at[side])
        from_side("t1", side, t1h.at[side])
        from_side("c2", side, c2h.at[side])
        own, beyond = m2e[i + 1], m2e[end]
        rest = c[end] * (own + inplane(beyond)) + react(beyond, t1h[side]) + c2h[side] * beyond
        more = 8 * W24 * c[end] * m1e[i + 1] - W24 * rest
        dE[side * (cn + 1)] = unfold(dwh[side]) + 0.25 * pair(more)

    def final_fast(j):
        jE[j] += coarse_step(j, m1e, dE[j] + dE[j + 2])

    each(0, cn, final_fast)
    for row in (0, 1):
        store(jE, jump_out.at[0, :, row])

    for name, src, dst, when, dp, dside in pending:

        @pl.when(when)
        def _():
            copy_of(name, src, dst, dp, dside).wait_send()

    for stored in stores:
        stored.wait()


def per_device(start, conduct, threshold, recovery):
    nx, ny, nz = conduct.shape
    cn = nx // 2

    def planes(count, rows=ny):
        return pltpu.VMEM((count, rows, nz), jnp.float32)

    own, padded, coarse, two, half = (
        planes(nx), planes(nx + 2), planes(cn), planes(2), planes(2, ny // 2)
    )
    scratch = [
        padded, own, padded, own, own, coarse, coarse, coarse,
        own, own, padded, own, padded, own, own, own,
        planes(cn + 2), coarse, coarse, coarse, padded, padded, own, own, own, own,
        padded, own, padded, own, padded, own, own, own,
        two, two, half, half, half, half, half, two, own, own, coarse, coarse,
        two, two, half, half, two, two,
        pltpu.SemaphoreType.DMA((5,)),
        pltpu.SemaphoreType.DMA((6,)),
        pltpu.SemaphoreType.DMA((len(MESSAGES),)),
        pltpu.SemaphoreType.DMA((len(MESSAGES),)),
    ]
    nodes, jumps = pl.pallas_call(
        kernel,
        out_shape=[
            jax.ShapeDtypeStruct((2, nx, ny, nz), jnp.float32),
            jax.ShapeDtypeStruct((2, cn, 2, ny, nz), jnp.float32),
        ],
        in_specs=[pl.BlockSpec(memory_space=pl.ANY)] * 4,
        out_specs=[pl.BlockSpec(memory_space=pl.ANY)] * 2,
        scratch_shapes=scratch,
        compiler_params=pltpu.CompilerParams(
            collective_id=0, has_side_effects=True, vmem_limit_bytes=62 * 1024 * 1024
        ),
    )(start, conduct, threshold, recovery)
    return (nodes + jumps.reshape(2, nx, ny, nz)).reshape(start.shape)


def solution(mesh):
    placed = (
        P("tm", None, "space", None, None),
        P("space", None, None),
        P("space", None, None),
        P("space", None, None),
    )
    return jax.shard_map(
        per_device,
        mesh=mesh,
        in_specs=placed,
        out_specs=P("tm", None, "space", None, None),
        check_vma=False,
    )
```

```python
import functools
import jax
import jax.numpy as jnp
from jax import lax
from jax.experimental import pallas as pl
from jax.experimental.pallas import tpu as pltpu
from jax.sharding import PartitionSpec as P

MESH = pl.DeviceIdType.MESH
SIXTH = 1.0 / 6.0
W24 = 1.0 / 24.0


def react(e, t):
    return 2.0 * e * (1.0 - e) * (e - t)


def near(v, axis, by):
    if axis == 0:
        rows, lanes = v.shape
        groups = v.reshape(rows // 8, 8, lanes)
        at = lax.broadcasted_iota(jnp.int32, groups.shape, 1)
        none = jnp.zeros((1, 8, lanes), v.dtype)
        low = pltpu.roll(groups, by, 1)
        low = jnp.where(at < by, jnp.concatenate([none, low[:-1]], axis=0), low)
        high = pltpu.roll(groups, 8 - by, 1)
        high = jnp.where(at >= 8 - by, jnp.concatenate([high[1:], none], axis=0), high)
        return (low + high).reshape(rows, lanes)
    n = v.shape[axis]
    at = lax.broadcasted_iota(jnp.int32, v.shape, axis)
    low = jnp.where(at < by, 0.0, pltpu.roll(v, by, axis))
    high = jnp.where(at >= n - by, 0.0, pltpu.roll(v, n - by, axis))
    return low + high


def tiles(v, by):
    rows, lanes = v.shape
    return pltpu.roll(v.reshape(rows // 8, 8, lanes), by, 1).reshape(rows, lanes)


def even_rows(v):
    return lax.broadcasted_iota(jnp.int32, v.shape, 0) % 2 == 0


def pair(v):
    return v + jnp.where(even_rows(v), tiles(v, 7), tiles(v, 1))


def fold(v):
    half = v.shape[0] // 2
    return jnp.where(even_rows(v[:half]), v[:half], v[half:])


def expand(x):
    even = even_rows(x)
    return jnp.where(even, x, tiles(x, 1)), jnp.where(even, tiles(x, 7), x)


def unfold(x):
    return jnp.concatenate(expand(x), axis=0)


def inplane(e):
    return near(e, 0, 1) + near(e, 1, 1) - 6.0 * e


MESSAGES = {
    name: at
    for at, name in enumerate(
        [
            (kind, side)
            for kind in ("q", "c", "n1p", "n2", "dp", "n2x", "j", "jx", "m1", "m2p", "dw", "t1", "c2")
            for side in (0, 1)
        ]
        + [(kind, side) for kind in ("n2r", "n2e", "jt") for side in (0, 1, 2)]
    )
}


def kernel(
    start, cond, thr, rec, out,
    qe, qr, c, t, k, cc, tc, kc,
    f0e, f0r, n1e, n1r, n2e, n2r, t1e, t1r,
    dE, dR, jE, jR, u1e, u2e, s1e, s1r, s2e, s2r,
    qne, qnr, m1e, m1r, m2e, m2r, t0e, t0r, oe, orr,
    n1s, n1h, ds, dh, js, jh, jxh, n2xh, rn2r, rn2e, jts, jth,
    m2s, m2h, dws, dwh, t1h, c2h,
    load_sem, store_sem, send_sem, recv_sem,
):
    nx = qr.shape[0]
    cn = nx // 2
    p, s = lax.axis_index("tm"), lax.axis_index("space")
    slices, slabs = lax.axis_size("tm"), lax.axis_size("space")
    head = p == 0
    has = (s > 0, s < slabs - 1)
    earlier, later = p > 0, p < slices - 1
    plane = qe.shape[1:]
    zeros = jnp.zeros(plane, jnp.float32)

    loads = [
        pltpu.make_async_copy(src, dst, load_sem.at[i])
        for i, (src, dst) in enumerate(
            [
                (start.at[0, 0], qe.at[pl.ds(1, nx)]),
                (cond, c.at[pl.ds(1, nx)]),
                (thr, t),
                (start.at[0, 1], qr),
                (rec, k),
            ]
        )
    ]
    for load in loads:
        load.start()

    barrier = pltpu.get_barrier_semaphore()

    def greet(when, dp, dside):
        @pl.when(when)
        def _():
            pl.semaphore_signal(barrier, inc=1, device_id=(p + dp, s + dside), device_id_type=MESH)

    greet(has[0], 0, -1)
    greet(has[1], 0, 1)
    greet(earlier, -1, 0)
    greet(earlier & has[0], -1, -1)
    greet(earlier & has[1], -1, 1)

    for side in (0, 1):
        end = side * (nx + 1)

        @pl.when(jnp.logical_not(has[side]))
        def _():
            for ref in (qe, c):
                ref[end] = zeros
            for ref in (n1h, n2xh, m2h, t1h, c2h):
                ref[side] = zeros
            n2e[end] = zeros
            m1e[end] = zeros
            for ref in (dh, jh, jxh, dwh):
                ref[side] = zeros[: plane[0] // 2]

    sides = has[0].astype(jnp.int32) + has[1].astype(jnp.int32)
    after = later.astype(jnp.int32)
    pl.semaphore_wait(barrier, sides + after * (sides + 1))

    pending = []

    def copy_of(name, src, dst, dp, dside):
        at = MESSAGES[name]
        return pltpu.make_async_remote_copy(
            src_ref=src,
            dst_ref=dst,
            send_sem=send_sem.at[at],
            recv_sem=recv_sem.at[at],
            device_id=(p + dp, s + dside),
            device_id_type=MESH,
        )

    def send(name, src, dst, when, dp=0, dside=0):
        @pl.when(when)
        def _():
            copy_of(name, src, dst, dp, dside).start()

        pending.append((name, src, dst, when, dp, dside))

    def receive(name, dst, when):
        @pl.when(when)
        def _():
            copy_of(name, dst, dst, 0, 0).wait_recv()

    def to_sides(kind, src, dst):
        for side in (0, 1):
            send((kind, side), src(side), dst(1 - side), has[side], 0, 2 * side - 1)

    def to_later_sides(kind, src, dst):
        for side in (0, 1):
            send((kind, side), src(side), dst(1 - side), later & has[side], 1, 2 * side - 1)

    def from_side(kind, side, dst, when=None):
        receive((kind, 1 - side), dst, has[side] if when is None else when & has[side])

    def edge(side):
        return side * (nx - 1)

    def halo(ref):
        return lambda side: ref.at[side * (ref.shape[0] - 1)]

    def slot(ref):
        return lambda side: ref.at[side]

    def each(low, high, body):
        for i in range(low, high):
            body(i)

    def on_edges(body):
        each(0, 2, lambda side: body(side, side * (nx - 1), 2 + side * (nx - 3)))

    to_sides("q", lambda side: start.at[0, 0, edge(side)], halo(qe))
    to_sides("c", lambda side: cond.at[edge(side)], halo(c))
    for load in loads:
        load.wait()

    def first_edge(side, i, inner):
        e, r = qe[i + 1], qr[i]
        f = c[i + 1] * (qe[inner] + inplane(e)) + react(e, t[i]) - r
        g = k[i] * (e - 0.5 * r)
        f0e[i], f0r[i] = f, g
        n1 = e + 0.5 * f
        n1e[i + 1], n1s[side], n1r[i] = n1, n1, r + 0.5 * g

    on_edges(first_edge)
    to_sides("n1p", slot(n1s), slot(n1h))

    def slow_step(i):
        g = k[i] * (n1e[i + 1] - 0.5 * n1r[i])
        t1r[i] = g
        n2r[i] = n1r[i] + 0.5 * g

    def first_inner(i):
        e, r = qe[i + 1], qr[i]
        f = c[i + 1] * (qe[i] + qe[i + 2] + inplane(e)) + react(e, t[i]) - r
        g = k[i] * (e - 0.5 * r)
        f0e[i], f0r[i] = f, g
        n1e[i + 1], n1r[i] = e + 0.5 * f, r + 0.5 * g
        slow_step(i)

    each(1, nx - 1, first_inner)

    def hand_over(kind, part, ref, shift, dst, low, count):
        src = ref.at[pl.ds(low + shift, count)]
        send((kind, part), src, dst.at[pl.ds(low, count)], later, 1)

    hand_over("n2r", 2, n2r, 0, rn2r, 1, nx - 2)

    def second(i):
        e = n1e[i + 1]
        f = c[i + 1] * (n1e[i] + n1e[i + 2] + inplane(e)) + react(e, t[i]) - n1r[i]
        t1e[i] = f
        n2e[i + 1] = e + 0.5 * f

    each(2, nx - 2, second)
    hand_over("n2e", 2, n2e, 1, rn2e, 2, nx - 4)

    def coarse_coeffs(j):
        for fine, shift, coarse in ((c, 1, cc), (t, 0, tc), (k, 0, kc)):
            coarse[j] = 0.25 * pair(fine[2 * j + shift] + fine[2 * j + 1 + shift])

    each(0, cn, coarse_coeffs)

    for side in (0, 1):
        i, end = edge(side), side * (nx + 1)
        from_side("q", side, qe.at[end])
        from_side("c", side, c.at[end])
        from_side("n1p", side, n1h.at[side])
        more = c[i + 1] * qe[end]
        f0e[i] += more
        n1e[i + 1] += 0.5 * more
        n1e[end] = n1h[side] + 0.5 * c[end] * qe[i + 1]
        slow_step(i)

    on_edges(lambda side, i, inner: second(i))
    own_edge = lambda ref: lambda side: ref.at[edge(side) + 1]
    to_sides("n2", own_edge(n2e), halo(n2e))
    on_edges(lambda side, i, inner: second(inner - 1))
    for side in (0, 1):
        hand_over("n2e", side, n2e, 1, rn2e, side * (nx - 2), 2)
        hand_over("n2r", side, n2r, 0, rn2r, edge(side), 1)

    def third(j, e_ref, r_ref, extra, missing=None):
        sums = [0.0, 0.0, 0.0, 0.0]
        for row in (0, 1):
            i = 2 * j + row
            e, r = e_ref[i + 1], r_ref[i]
            if missing == 0 and row == 0:
                x = e_ref[i + 2]
            elif missing == 1 and row == 1:
                x = e_ref[i]
            else:
                x = e_ref[i] + e_ref[i + 2]
            fe = c[i + 1] * (x + inplane(e)) + react(e, t[i]) - r
            fr = k[i] * (e - 0.5 * r)
            a, b, g, h = extra(i)
            sums[0] += a - W24 * fe
            sums[1] += b - W24 * fr
            sums[2] += g + SIXTH * fe
            sums[3] += h + SIXTH * fr
        dE[j + 1] = 0.25 * pair(sums[0])
        dR[j] = 0.25 * pair(sums[1])
        jE[j] = 0.25 * pair(sums[2])
        jR[j] = 0.25 * pair(sums[3])

    def extra_first(i):
        a, b, g, h = f0e[i], t1e[i], f0r[i], t1r[i]
        return (
            8 * W24 * b - 7 * W24 * a,
            8 * W24 * h - 7 * W24 * g,
            SIXTH * b - 2 * SIXTH * a,
            SIXTH * h - 2 * SIXTH * g,
        )

    for side in (0, 1):
        third(side * (cn - 1), n2e, n2r, extra_first, side)
        ds[side] = fold(dE[side * (cn - 1) + 1])
    to_sides("dp", slot(ds), slot(dh))
    to_later_sides("n2x", own_edge(n2e), slot(n2xh))
    each(1, cn - 1, lambda j: third(j, n2e, n2r, extra_first))

    def coarse_step(j, node, x):
        d, dr = dE[j + 1], dR[j]
        lap = 0.25 * (x + near(d, 0, 2)) + near(d, 1, 1) - 3.0 * d
        b = 0.25 * pair(node[2 * j + 1] + node[2 * j + 2])
        return 0.5 * (cc[j] * lap + react(b + d, tc[j]) - react(b, tc[j]) - dr)

    def coarse_slow(j):
        return jR[j] + 0.5 * kc[j] * (dE[j + 1] - 0.5 * dR[j])

    def coarse_first(j):
        e = jE[j] + coarse_step(j, n1e, dE[j] + dE[j + 2])
        r = coarse_slow(j)
        jE[j], jR[j] = e, r
        jts[j] = jnp.where(even_rows(e), e, r)

    each(1, cn - 1, coarse_first)
    send(("jt", 2), jts.at[pl.ds(1, cn - 2)], jth.at[pl.ds(1, cn - 2)], later, 1)

    for side in (0, 1):
        i, j, end = edge(side), side * (cn - 1), side * (nx + 1)
        from_side("n2", side, n2e.at[end])
        from_side("dp", side, dh.at[side])
        more = 0.25 * pair(c[i + 1] * n2e[end])
        change = W24 * more
        dE[j + 1] -= change
        beside = 1 + side * (cn - 3)
        jE[beside] -= 0.125 * cc[beside] * change
        jE[j] += SIXTH * more
        dE[side * (cn + 1)] = unfold(dh[side]) - (0.25 * W24) * pair(c[end] * n2e[i + 1])

    each(0, 2, lambda side: coarse_first(side * (cn - 1)))
    for side in (0, 1):
        js[side] = fold(jE[side * (cn - 1)])
    to_sides("j", slot(js), slot(jh))
    to_later_sides("jx", slot(js), slot(jxh))
    for side in (0, 1):
        last = pl.ds(side * (cn - 1), 1)
        send(("jt", side), jts.at[last], jth.at[last], later, 1)

    to_sides("t1", lambda side: thr.at[edge(side)], slot(t1h))
    to_sides("c2", lambda side: cond.at[1 + side * (nx - 3)], slot(c2h))

    def correct(j):
        for row in (0, 1):
            i = 2 * j + row
            u1e[i + 1] = n1e[i + 1] + dE[j + 1]
            u2e[i + 1] = n2e[i + 1] + jE[j]

    each(0, cn, correct)
    for side in (0, 1):
        end = side * (nx + 1)
        u1e[end] = n1e[end] + dE[side * (cn + 1)]
        u2e[end] = zeros

    def old_terms(j):
        for row in (0, 1):
            i = 2 * j + row
            u1, u2 = u1e[i + 1], u2e[i + 1]
            u1r, u2r = n1r[i] + dR[j], n2r[i] + jR[j]
            a1 = c[i + 1] * (u1e[i] + u1e[i + 2] + inplane(u1)) + react(u1, t[i]) - u1r
            a2 = c[i + 1] * (u2e[i] + u2e[i + 2] + inplane(u2)) + react(u2, t[i]) - u2r
            b1 = k[i] * (u1 - 0.5 * u1r)
            b2 = k[i] * (u2 - 0.5 * u2r)
            a0, b0 = f0e[i], f0r[i]
            s1e[i] = 8 * W24 * a1 - 7 * W24 * a0 - W24 * a2
            s1r[i] = 8 * W24 * b1 - 7 * W24 * b0 - W24 * b2
            s2e[i] = 5 * W24 * a2 - W24 * a0 - 4 * W24 * a1
            s2r[i] = 5 * W24 * b2 - W24 * b0 - 4 * W24 * b1

    each(0, cn, old_terms)

    for side in (0, 1):
        i, end = edge(side), side * (nx + 1)
        from_side("j", side, jh.at[side])
        more = c[i + 1] * (n2e[end] + unfold(jh[side]))
        s1e[i] -= W24 * more
        s2e[i] += 5 * W24 * more

    receive(("n2r", 2), rn2r.at[pl.ds(1, nx - 2)], earlier)
    receive(("n2e", 2), rn2e.at[pl.ds(2, nx - 4)], earlier)
    for side in (0, 1):
        receive(("n2r", side), rn2r.at[pl.ds(edge(side), 1)], earlier)
        receive(("n2e", side), rn2e.at[pl.ds(side * (nx - 2), 2)], earlier)
    for side in (0, 1):
        from_side("n2x", side, n2xh.at[side], earlier)
        from_side("jx", side, jxh.at[side], earlier)
        end = side * (nx + 1)
        qne[end] = jnp.where(head, qe[end], n2xh[side] + unfold(jxh[side]))
    receive(("jt", 2), jth.at[pl.ds(1, cn - 2)], earlier)
    for side in (0, 1):
        receive(("jt", side), jth.at[pl.ds(side * (cn - 1), 1)], earlier)

    def arrive(j, side=None):
        e, r = expand(jth[j])
        if side is not None:
            e -= (0.125 * W24 * 0.25) * cc[j] * pair(c[edge(side) + 1] * n2xh[side])
        for row in (0, 1):
            i = 2 * j + row
            qne[i + 1] = jnp.where(head, qe[i + 1], rn2e[i] + e)
            qnr[i] = jnp.where(head, qr[i], rn2r[i] + r)

    each(0, 2, lambda side: arrive(side * (cn - 1)))
    for side in (0, 1):
        arrive(1 + side * (cn - 3), side)
    each(2, cn - 2, arrive)

    def next_first(i):
        e, r = qne[i + 1], qnr[i]
        f = c[i + 1] * (qne[i] + qne[i + 2] + inplane(e)) + react(e, t[i]) - r
        g = k[i] * (e - 0.5 * r)
        t0e[i], t0r[i] = f, g
        m1e[i + 1] = e + 0.5 * f + s1e[i]
        m1r[i] = r + 0.5 * g + s1r[i]

    on_edges(lambda side, i, inner: next_first(i))
    to_sides("m1", own_edge(m1e), halo(m1e))
    on_edges(lambda side, i, inner: next_first(inner - 1))

    def next_second(i, x):
        e, r = m1e[i + 1], m1r[i]
        f = c[i + 1] * (x + inplane(e)) + react(e, t[i]) - r
        g = k[i] * (e - 0.5 * r)
        t1e[i], t1r[i] = f, g
        m2 = e + 0.5 * f + s2e[i]
        m2e[i + 1] = m2
        m2r[i] = r + 0.5 * g + s2r[i]
        return m2

    def next_edge(side, i, inner):
        m2s[side] = next_second(i, m1e[inner])

    on_edges(next_edge)
    to_sides("m2p", slot(m2s), slot(m2h))
    each(2, nx - 2, next_first)
    each(1, nx - 1, lambda i: next_second(i, m1e[i] + m1e[i + 2]))

    def defect(i):
        return 8 * W24 * t1e[i] - 7 * W24 * t0e[i] - s1e[i]

    def next_defect(side, i, inner):
        second, third_at = inner - 1, 2 + side * (nx - 5)
        e = m2e[second + 1]
        rest = c[second + 1] * (m2e[third_at + 1] + inplane(e)) + react(e, t[second])
        rest = rest - m2r[second] - m2r[i] + c[i + 1] * e
        dws[side] = fold(0.25 * pair(defect(i) + defect(second) - W24 * rest))

    on_edges(next_defect)
    to_sides("dw", slot(dws), slot(dwh))

    for side in (0, 1):
        i, end = edge(side), side * (nx + 1)
        from_side("m1", side, m1e.at[end])
        from_side("m2p", side, m2h.at[side])
        more = c[i + 1] * m1e[end]
        t1e[i] += more
        m2e[i + 1] += 0.5 * more
        m2e[end] = m2h[side] + 0.5 * c[end] * m1e[i + 1]

    stores = []

    def store(src, dst):
        stores.append(pltpu.make_async_copy(src, dst, store_sem.at[len(stores)]))
        stores[-1].start()

    def extra_next(i):
        a, b, g, h = t0e[i], t1e[i], t0r[i], t1r[i]
        return (
            8 * W24 * b - 7 * W24 * a - s1e[i],
            8 * W24 * h - 7 * W24 * g - s1r[i],
            SIXTH * b - 2 * SIXTH * a - s1e[i] - s2e[i],
            SIXTH * h - 2 * SIXTH * g - s1r[i] - s2r[i],
        )

    each(0, cn, lambda j: third(j, m2e, m2r, extra_next))

    def final_slow(j):
        r = coarse_slow(j)
        for row in (0, 1):
            orr[2 * j + row] = m2r[2 * j + row] + r

    each(0, cn, final_slow)
    store(orr, out.at[0, 1])

    for side in (0, 1):
        i, end = edge(side), side * (nx + 1)
        from_side("dw", side, dwh.at[side])
        from_side("t1", side, t1h.at[side])
        from_side("c2", side, c2h.at[side])
        own, beyond = m2e[i + 1], m2e[end]
        rest = c[end] * (own + inplane(beyond)) + react(beyond, t1h[side]) + c2h[side] * beyond
        more = 8 * W24 * c[end] * m1e[i + 1] - W24 * rest
        dE[side * (cn + 1)] = unfold(dwh[side]) + 0.25 * pair(more)

    def final_fast(j):
        e = jE[j] + coarse_step(j, m1e, dE[j] + dE[j + 2])
        for row in (0, 1):
            oe[2 * j + row] = m2e[2 * j + 1 + row] + e

    each(0, cn, final_fast)
    store(oe, out.at[0, 0])

    for name, src, dst, when, dp, dside in pending:

        @pl.when(when)
        def _():
            copy_of(name, src, dst, dp, dside).wait_send()

    for stored in stores:
        stored.wait()


def per_device(start, conduct, threshold, recovery):
    nx, ny, nz = conduct.shape
    cn = nx // 2

    def planes(count, rows=ny):
        return pltpu.VMEM((count, rows, nz), jnp.float32)

    own, padded, coarse, two, half = (
        planes(nx), planes(nx + 2), planes(cn), planes(2), planes(2, ny // 2)
    )
    scratch = [
        padded, own, padded, own, own, coarse, coarse, coarse,
        own, own, padded, own, padded, own, own, own,
        planes(cn + 2), coarse, coarse, coarse, padded, padded, own, own, own, own,
        padded, own, padded, own, padded, own, own, own, own, own,
        two, two, half, half, half, half, half, two, own, own, coarse, coarse,
        two, two, half, half, two, two,
        pltpu.SemaphoreType.DMA((5,)),
        pltpu.SemaphoreType.DMA((6,)),
        pltpu.SemaphoreType.DMA((len(MESSAGES),)),
        pltpu.SemaphoreType.DMA((len(MESSAGES),)),
    ]
    return pl.pallas_call(
        kernel,
        out_shape=jax.ShapeDtypeStruct(start.shape, jnp.float32),
        in_specs=[pl.BlockSpec(memory_space=pl.ANY)] * 4,
        out_specs=pl.BlockSpec(memory_space=pl.ANY),
        scratch_shapes=scratch,
        compiler_params=pltpu.CompilerParams(
            collective_id=0, has_side_effects=True, vmem_limit_bytes=62 * 1024 * 1024
        ),
    )(start, conduct, threshold, recovery)


def solution(mesh):
    placed = (
        P("tm", None, "space", None, None),
        P("space", None, None),
        P("space", None, None),
        P("space", None, None),
    )
    return jax.shard_map(
        per_device,
        mesh=mesh,
        in_specs=placed,
        out_specs=P("tm", None, "space", None, None),
        check_vma=False,
    )
```

```python
import functools
import jax
import jax.numpy as jnp
from jax import lax
from jax.experimental import pallas as pl
from jax.experimental.pallas import tpu as pltpu
from jax.sharding import PartitionSpec as P

MESH = pl.DeviceIdType.MESH
SIXTH = 1.0 / 6.0
W24 = 1.0 / 24.0


def react(e, t):
    return 2.0 * e * (1.0 - e) * (e - t)


def near(v, axis, by):
    if axis == 0:
        rows, lanes = v.shape
        groups = v.reshape(rows // 8, 8, lanes)
        at = lax.broadcasted_iota(jnp.int32, groups.shape, 1)
        none = jnp.zeros((1, 8, lanes), v.dtype)
        low = pltpu.roll(groups, by, 1)
        low = jnp.where(at < by, jnp.concatenate([none, low[:-1]], axis=0), low)
        high = pltpu.roll(groups, 8 - by, 1)
        high = jnp.where(at >= 8 - by, jnp.concatenate([high[1:], none], axis=0), high)
        return (low + high).reshape(rows, lanes)
    n = v.shape[axis]
    at = lax.broadcasted_iota(jnp.int32, v.shape, axis)
    low = jnp.where(at < by, 0.0, pltpu.roll(v, by, axis))
    high = jnp.where(at >= n - by, 0.0, pltpu.roll(v, n - by, axis))
    return low + high


def tiles(v, by):
    rows, lanes = v.shape
    return pltpu.roll(v.reshape(rows // 8, 8, lanes), by, 1).reshape(rows, lanes)


def even_rows(v):
    return lax.broadcasted_iota(jnp.int32, v.shape, 0) % 2 == 0


def pair(v):
    return v + jnp.where(even_rows(v), tiles(v, 7), tiles(v, 1))


def fold(v):
    half = v.shape[0] // 2
    return jnp.where(even_rows(v[:half]), v[:half], v[half:])


def expand(x):
    even = even_rows(x)
    return jnp.where(even, x, tiles(x, 1)), jnp.where(even, tiles(x, 7), x)


def unfold(x):
    return jnp.concatenate(expand(x), axis=0)


def inplane(e):
    return near(e, 0, 1) + near(e, 1, 1) - 6.0 * e


MESSAGES = {
    name: at
    for at, name in enumerate(
        [
            (kind, side)
            for kind in ("q", "c", "n1p", "n2", "dp", "n2x", "j", "jx", "m1", "m2p", "dw", "t1", "c2")
            for side in (0, 1)
        ]
        + [(kind, side) for kind in ("n2r", "n2e", "jt") for side in (0, 1, 2)]
    )
}


def kernel(
    start, cond, thr, rec, out,
    qe, qr, c, t, k, cc, tc, kc,
    f0e, f0r, n1e, n1r, n2e, n2r, t1e, t1r,
    dE, dR, jE, jR, u1e, u2e, s1e, s1r, s2e, s2r,
    qne, qnr, m1e, m1r, m2e, m2r, t0e, t0r, oe, orr,
    n1s, n1h, ds, dh, js, jh, jxh, n2xh, rn2r, rn2e, jts, jth,
    m2s, m2h, dws, dwh, t1h, c2h,
    load_sem, store_sem, send_sem, recv_sem,
):
    nx = qr.shape[0]
    cn = nx // 2
    p, s = lax.axis_index("tm"), lax.axis_index("space")
    slices, slabs = lax.axis_size("tm"), lax.axis_size("space")
    head = p == 0
    has = (s > 0, s < slabs - 1)
    earlier, later = p > 0, p < slices - 1
    plane = qe.shape[1:]
    zeros = jnp.zeros(plane, jnp.float32)

    loads = [
        pltpu.make_async_copy(src, dst, load_sem.at[i])
        for i, (src, dst) in enumerate(
            [
                (start.at[0, 0], qe.at[pl.ds(1, nx)]),
                (cond, c.at[pl.ds(1, nx)]),
                (thr, t),
                (start.at[0, 1], qr),
                (rec, k),
            ]
        )
    ]
    for load in loads:
        load.start()

    barrier = pltpu.get_barrier_semaphore()

    def greet(when, dp, dside):
        @pl.when(when)
        def _():
            pl.semaphore_signal(barrier, inc=1, device_id=(p + dp, s + dside), device_id_type=MESH)

    greet(has[0], 0, -1)
    greet(has[1], 0, 1)
    greet(earlier, -1, 0)
    greet(earlier & has[0], -1, -1)
    greet(earlier & has[1], -1, 1)

    for side in (0, 1):
        end = side * (nx + 1)

        @pl.when(jnp.logical_not(has[side]))
        def _():
            for ref in (qe, c):
                ref[end] = zeros
            for ref in (n1h, n2xh, m2h, t1h, c2h):
                ref[side] = zeros
            n2e[end] = zeros
            m1e[end] = zeros
            for ref in (dh, jh, jxh, dwh):
                ref[side] = zeros[: plane[0] // 2]

    sides = has[0].astype(jnp.int32) + has[1].astype(jnp.int32)
    after = later.astype(jnp.int32)
    pl.semaphore_wait(barrier, sides + after * (sides + 1))

    pending = []

    def copy_of(name, src, dst, dp, dside):
        at = MESSAGES[name]
        return pltpu.make_async_remote_copy(
            src_ref=src,
            dst_ref=dst,
            send_sem=send_sem.at[at],
            recv_sem=recv_sem.at[at],
            device_id=(p + dp, s + dside),
            device_id_type=MESH,
        )

    def send(name, src, dst, when, dp=0, dside=0):
        @pl.when(when)
        def _():
            copy_of(name, src, dst, dp, dside).start()

        pending.append((name, src, dst, when, dp, dside))

    def receive(name, dst, when):
        @pl.when(when)
        def _():
            copy_of(name, dst, dst, 0, 0).wait_recv()

    def to_sides(kind, src, dst):
        for side in (0, 1):
            send((kind, side), src(side), dst(1 - side), has[side], 0, 2 * side - 1)

    def to_later_sides(kind, src, dst):
        for side in (0, 1):
            send((kind, side), src(side), dst(1 - side), later & has[side], 1, 2 * side - 1)

    def from_side(kind, side, dst, when=None):
        receive((kind, 1 - side), dst, has[side] if when is None else when & has[side])

    def edge(side):
        return side * (nx - 1)

    def halo(ref):
        return lambda side: ref.at[side * (ref.shape[0] - 1)]

    def slot(ref):
        return lambda side: ref.at[side]

    def each(low, high, body):
        for i in range(low, high):
            body(i)

    def on_edges(body):
        each(0, 2, lambda side: body(side, side * (nx - 1), 2 + side * (nx - 3)))

    to_sides("q", lambda side: start.at[0, 0, edge(side)], halo(qe))
    to_sides("c", lambda side: cond.at[edge(side)], halo(c))
    for load in loads:
        load.wait()

    def first_edge(side, i, inner):
        e, r = qe[i + 1], qr[i]
        f = c[i + 1] * (qe[inner] + inplane(e)) + react(e, t[i]) - r
        g = k[i] * (e - 0.5 * r)
        f0e[i], f0r[i] = f, g
        n1 = e + 0.5 * f
        n1e[i + 1], n1s[side], n1r[i] = n1, n1, r + 0.5 * g

    on_edges(first_edge)
    to_sides("n1p", slot(n1s), slot(n1h))

    def slow_step(i):
        g = k[i] * (n1e[i + 1] - 0.5 * n1r[i])
        t1r[i] = g
        n2r[i] = n1r[i] + 0.5 * g

    def first_inner(i):
        e, r = qe[i + 1], qr[i]
        f = c[i + 1] * (qe[i] + qe[i + 2] + inplane(e)) + react(e, t[i]) - r
        g = k[i] * (e - 0.5 * r)
        f0e[i], f0r[i] = f, g
        n1e[i + 1], n1r[i] = e + 0.5 * f, r + 0.5 * g
        slow_step(i)

    each(1, nx - 1, first_inner)

    def hand_over(kind, part, ref, shift, dst, low, count):
        src = ref.at[pl.ds(low + shift, count)]
        send((kind, part), src, dst.at[pl.ds(low, count)], later, 1)

    hand_over("n2r", 2, n2r, 0, rn2r, 1, nx - 2)

    def second(i):
        e = n1e[i + 1]
        f = c[i + 1] * (n1e[i] + n1e[i + 2] + inplane(e)) + react(e, t[i]) - n1r[i]
        t1e[i] = f
        n2e[i + 1] = e + 0.5 * f

    each(2, nx - 2, second)
    hand_over("n2e", 2, n2e, 1, rn2e, 2, nx - 4)

    def coarse_coeffs(j):
        for fine, shift, coarse in ((c, 1, cc), (t, 0, tc), (k, 0, kc)):
            coarse[j] = 0.25 * pair(fine[2 * j + shift] + fine[2 * j + 1 + shift])

    each(0, cn, coarse_coeffs)

    for side in (0, 1):
        i, end = edge(side), side * (nx + 1)
        from_side("q", side, qe.at[end])
        from_side("c", side, c.at[end])
        from_side("n1p", side, n1h.at[side])
        more = c[i + 1] * qe[end]
        f0e[i] += more
        n1e[i + 1] += 0.5 * more
        n1e[end] = n1h[side] + 0.5 * c[end] * qe[i + 1]
        slow_step(i)

    on_edges(lambda side, i, inner: second(i))
    own_edge = lambda ref: lambda side: ref.at[edge(side) + 1]
    to_sides("n2", own_edge(n2e), halo(n2e))
    on_edges(lambda side, i, inner: second(inner - 1))
    for side in (0, 1):
        hand_over("n2e", side, n2e, 1, rn2e, side * (nx - 2), 2)
        hand_over("n2r", side, n2r, 0, rn2r, edge(side), 1)

    def third(j, e_ref, r_ref, extra, missing=None):
        sums = [0.0, 0.0, 0.0, 0.0]
        for row in (0, 1):
            i = 2 * j + row
            e, r = e_ref[i + 1], r_ref[i]
            if missing == 0 and row == 0:
                x = e_ref[i + 2]
            elif missing == 1 and row == 1:
                x = e_ref[i]
            else:
                x = e_ref[i] + e_ref[i + 2]
            fe = c[i + 1] * (x + inplane(e)) + react(e, t[i]) - r
            fr = k[i] * (e - 0.5 * r)
            a, b, g, h = extra(i)
            sums[0] += a - W24 * fe
            sums[1] += b - W24 * fr
            sums[2] += g + SIXTH * fe
            sums[3] += h + SIXTH * fr
        dE[j + 1] = 0.25 * pair(sums[0])
        dR[j] = 0.25 * pair(sums[1])
        jE[j] = 0.25 * pair(sums[2])
        jR[j] = 0.25 * pair(sums[3])

    def extra_first(i):
        a, b, g, h = f0e[i], t1e[i], f0r[i], t1r[i]
        return (
            8 * W24 * b - 7 * W24 * a,
            8 * W24 * h - 7 * W24 * g,
            SIXTH * b - 2 * SIXTH * a,
            SIXTH * h - 2 * SIXTH * g,
        )

    for side in (0, 1):
        third(side * (cn - 1), n2e, n2r, extra_first, side)
        ds[side] = fold(dE[side * (cn - 1) + 1])
    to_sides("dp", slot(ds), slot(dh))
    to_later_sides("n2x", own_edge(n2e), slot(n2xh))
    each(1, cn - 1, lambda j: third(j, n2e, n2r, extra_first))

    def coarse_step(j, node, x):
        d, dr = dE[j + 1], dR[j]
        lap = 0.25 * (x + near(d, 0, 2)) + near(d, 1, 1) - 3.0 * d
        b = 0.25 * pair(node[2 * j + 1] + node[2 * j + 2])
        return 0.5 * (cc[j] * lap + react(b + d, tc[j]) - react(b, tc[j]) - dr)

    def coarse_slow(j):
        return jR[j] + 0.5 * kc[j] * (dE[j + 1] - 0.5 * dR[j])

    def coarse_first(j):
        e = jE[j] + coarse_step(j, n1e, dE[j] + dE[j + 2])
        r = coarse_slow(j)
        jE[j], jR[j] = e, r
        jts[j] = jnp.where(even_rows(e), e, r)

    each(1, cn - 1, coarse_first)
    send(("jt", 2), jts.at[pl.ds(1, cn - 2)], jth.at[pl.ds(1, cn - 2)], later, 1)

    for side in (0, 1):
        i, j, end = edge(side), side * (cn - 1), side * (nx + 1)
        from_side("n2", side, n2e.at[end])
        from_side("dp", side, dh.at[side])
        more = 0.25 * pair(c[i + 1] * n2e[end])
        change = W24 * more
        dE[j + 1] -= change
        beside = 1 + side * (cn - 3)
        jE[beside] -= 0.125 * cc[beside] * change
        jE[j] += SIXTH * more
        dE[side * (cn + 1)] = unfold(dh[side]) - (0.25 * W24) * pair(c[end] * n2e[i + 1])

    each(0, 2, lambda side: coarse_first(side * (cn - 1)))
    for side in (0, 1):
        js[side] = fold(jE[side * (cn - 1)])
    to_sides("j", slot(js), slot(jh))
    to_later_sides("jx", slot(js), slot(jxh))
    for side in (0, 1):
        last = pl.ds(side * (cn - 1), 1)
        send(("jt", side), jts.at[last], jth.at[last], later, 1)

    to_sides("t1", lambda side: thr.at[edge(side)], slot(t1h))
    to_sides("c2", lambda side: cond.at[1 + side * (nx - 3)], slot(c2h))

    def correct(j):
        for row in (0, 1):
            i = 2 * j + row
            u1e[i + 1] = n1e[i + 1] + dE[j + 1]
            u2e[i + 1] = n2e[i + 1] + jE[j]

    each(0, cn, correct)
    for side in (0, 1):
        end = side * (nx + 1)
        u1e[end] = n1e[end] + dE[side * (cn + 1)]
        u2e[end] = zeros

    def old_terms(j):
        for row in (0, 1):
            i = 2 * j + row
            u1, u2 = u1e[i + 1], u2e[i + 1]
            u1r, u2r = n1r[i] + dR[j], n2r[i] + jR[j]
            a1 = c[i + 1] * (u1e[i] + u1e[i + 2] + inplane(u1)) + react(u1, t[i]) - u1r
            a2 = c[i + 1] * (u2e[i] + u2e[i + 2] + inplane(u2)) + react(u2, t[i]) - u2r
            b1 = k[i] * (u1 - 0.5 * u1r)
            b2 = k[i] * (u2 - 0.5 * u2r)
            a0, b0 = f0e[i], f0r[i]
            s1e[i] = 8 * W24 * a1 - 7 * W24 * a0 - W24 * a2
            s1r[i] = 8 * W24 * b1 - 7 * W24 * b0 - W24 * b2
            s2e[i] = 5 * W24 * a2 - W24 * a0 - 4 * W24 * a1
            s2r[i] = 5 * W24 * b2 - W24 * b0 - 4 * W24 * b1

    each(0, cn, old_terms)

    for side in (0, 1):
        i, end = edge(side), side * (nx + 1)
        from_side("j", side, jh.at[side])
        more = c[i + 1] * (n2e[end] + unfold(jh[side]))
        s1e[i] -= W24 * more
        s2e[i] += 5 * W24 * more

    receive(("n2r", 2), rn2r.at[pl.ds(1, nx - 2)], earlier)
    receive(("n2e", 2), rn2e.at[pl.ds(2, nx - 4)], earlier)
    for side in (0, 1):
        receive(("n2r", side), rn2r.at[pl.ds(edge(side), 1)], earlier)
        receive(("n2e", side), rn2e.at[pl.ds(side * (nx - 2), 2)], earlier)
    for side in (0, 1):
        from_side("n2x", side, n2xh.at[side], earlier)
        from_side("jx", side, jxh.at[side], earlier)
        end = side * (nx + 1)
        qne[end] = jnp.where(head, qe[end], n2xh[side] + unfold(jxh[side]))
    receive(("jt", 2), jth.at[pl.ds(1, cn - 2)], earlier)
    for side in (0, 1):
        receive(("jt", side), jth.at[pl.ds(side * (cn - 1), 1)], earlier)

    def arrive(j, side=None):
        e, r = expand(jth[j])
        if side is not None:
            e -= (0.125 * W24 * 0.25) * cc[j] * pair(c[edge(side) + 1] * n2xh[side])
        for row in (0, 1):
            i = 2 * j + row
            qne[i + 1] = jnp.where(head, qe[i + 1], rn2e[i] + e)
            qnr[i] = jnp.where(head, qr[i], rn2r[i] + r)

    each(0, 2, lambda side: arrive(side * (cn - 1)))
    for side in (0, 1):
        arrive(1 + side * (cn - 3), side)
    each(2, cn - 2, arrive)

    def next_first(i):
        e, r = qne[i + 1], qnr[i]
        f = c[i + 1] * (qne[i] + qne[i + 2] + inplane(e)) + react(e, t[i]) - r
        g = k[i] * (e - 0.5 * r)
        t0e[i], t0r[i] = f, g
        m1e[i + 1] = e + 0.5 * f + s1e[i]
        m1r[i] = r + 0.5 * g + s1r[i]

    on_edges(lambda side, i, inner: next_first(i))
    to_sides("m1", own_edge(m1e), halo(m1e))
    on_edges(lambda side, i, inner: next_first(inner - 1))

    def next_second(i, x):
        e, r = m1e[i + 1], m1r[i]
        f = c[i + 1] * (x + inplane(e)) + react(e, t[i]) - r
        g = k[i] * (e - 0.5 * r)
        t1e[i], t1r[i] = f, g
        m2 = e + 0.5 * f + s2e[i]
        m2e[i + 1] = m2
        m2r[i] = r + 0.5 * g + s2r[i]
        return m2

    def next_edge(side, i, inner):
        m2s[side] = next_second(i, m1e[inner])

    on_edges(next_edge)
    to_sides("m2p", slot(m2s), slot(m2h))
    each(2, nx - 2, next_first)
    for i in sorted({1, 2, nx - 3, nx - 2}):
        next_second(i, m1e[i] + m1e[i + 2])

    def defect(i):
        return 8 * W24 * t1e[i] - 7 * W24 * t0e[i] - s1e[i]

    def next_defect(side, i, inner):
        second, third_at = inner - 1, 2 + side * (nx - 5)
        e = m2e[second + 1]
        rest = c[second + 1] * (m2e[third_at + 1] + inplane(e)) + react(e, t[second])
        rest = rest - m2r[second] - m2r[i] + c[i + 1] * e
        dws[side] = fold(0.25 * pair(defect(i) + defect(second) - W24 * rest))

    on_edges(next_defect)
    to_sides("dw", slot(dws), slot(dwh))
    each(3, nx - 3, lambda i: next_second(i, m1e[i] + m1e[i + 2]))

    for side in (0, 1):
        i, end = edge(side), side * (nx + 1)
        from_side("m1", side, m1e.at[end])
        from_side("m2p", side, m2h.at[side])
        more = c[i + 1] * m1e[end]
        t1e[i] += more
        m2e[i + 1] += 0.5 * more
        m2e[end] = m2h[side] + 0.5 * c[end] * m1e[i + 1]

    stores = []

    def store(src, dst):
        stores.append(pltpu.make_async_copy(src, dst, store_sem.at[len(stores)]))
        stores[-1].start()

    def extra_next(i):
        a, b, g, h = t0e[i], t1e[i], t0r[i], t1r[i]
        return (
            8 * W24 * b - 7 * W24 * a - s1e[i],
            8 * W24 * h - 7 * W24 * g - s1r[i],
            SIXTH * b - 2 * SIXTH * a - s1e[i] - s2e[i],
            SIXTH * h - 2 * SIXTH * g - s1r[i] - s2r[i],
        )

    each(0, cn, lambda j: third(j, m2e, m2r, extra_next))

    def final_slow(j):
        r = coarse_slow(j)
        for row in (0, 1):
            orr[2 * j + row] = m2r[2 * j + row] + r

    each(0, cn, final_slow)
    store(orr, out.at[0, 1])

    for side in (0, 1):
        i, end = edge(side), side * (nx + 1)
        from_side("dw", side, dwh.at[side])
        from_side("t1", side, t1h.at[side])
        from_side("c2", side, c2h.at[side])
        own, beyond = m2e[i + 1], m2e[end]
        rest = c[end] * (own + inplane(beyond)) + react(beyond, t1h[side]) + c2h[side] * beyond
        more = 8 * W24 * c[end] * m1e[i + 1] - W24 * rest
        dE[side * (cn + 1)] = unfold(dwh[side]) + 0.25 * pair(more)

    def final_fast(j):
        e = jE[j] + coarse_step(j, m1e, dE[j] + dE[j + 2])
        for row in (0, 1):
            oe[2 * j + row] = m2e[2 * j + 1 + row] + e

    each(0, cn, final_fast)
    store(oe, out.at[0, 0])

    for name, src, dst, when, dp, dside in pending:

        @pl.when(when)
        def _():
            copy_of(name, src, dst, dp, dside).wait_send()

    for stored in stores:
        stored.wait()


def place(src, dst, held, load_sem, store_sem):
    parts = [(field, i) for field in range(src.shape[1]) for i in range(0, src.shape[2], 2)]
    loads, stores = [], []
    for at, (field, i) in enumerate(parts):
        here = held.at[field, pl.ds(i, 2)]
        loads.append(pltpu.make_async_copy(src.at[0, field, pl.ds(i, 2)], here, load_sem.at[at]))
        stores.append(pltpu.make_async_copy(here, dst.at[0, field, pl.ds(i, 2)], store_sem.at[at]))
        loads[-1].start()
    for load, store in zip(loads, stores):
        load.wait()
        store.start()
    for store in stores:
        store.wait()


def per_device(start, conduct, threshold, recovery):
    nx, ny, nz = conduct.shape
    cn = nx // 2

    def planes(count, rows=ny):
        return pltpu.VMEM((count, rows, nz), jnp.float32)

    own, padded, coarse, two, half = (
        planes(nx), planes(nx + 2), planes(cn), planes(2), planes(2, ny // 2)
    )
    scratch = [
        padded, own, padded, own, own, coarse, coarse, coarse,
        own, own, padded, own, padded, own, own, own,
        planes(cn + 2), coarse, coarse, coarse, padded, padded, own, own, own, own,
        padded, own, padded, own, padded, own, own, own, own, own,
        two, two, half, half, half, half, half, two, own, own, coarse, coarse,
        two, two, half, half, two, two,
        pltpu.SemaphoreType.DMA((5,)),
        pltpu.SemaphoreType.DMA((6,)),
        pltpu.SemaphoreType.DMA((len(MESSAGES),)),
        pltpu.SemaphoreType.DMA((len(MESSAGES),)),
    ]
    result = pl.pallas_call(
        kernel,
        out_shape=jax.ShapeDtypeStruct(start.shape, jnp.float32),
        in_specs=[pl.BlockSpec(memory_space=pl.ANY)] * 4,
        out_specs=pl.BlockSpec(memory_space=pl.ANY),
        scratch_shapes=scratch,
        compiler_params=pltpu.CompilerParams(
            collective_id=0, has_side_effects=True, vmem_limit_bytes=62 * 1024 * 1024
        ),
    )(start, conduct, threshold, recovery)
    return pl.pallas_call(
        place,
        out_shape=jax.ShapeDtypeStruct(start.shape, jnp.float32),
        in_specs=[pl.BlockSpec(memory_space=pl.ANY)],
        out_specs=pl.BlockSpec(memory_space=pl.ANY),
        scratch_shapes=[
            pltpu.VMEM(start.shape[1:], jnp.float32),
            pltpu.SemaphoreType.DMA((nx,)),
            pltpu.SemaphoreType.DMA((nx,)),
        ],
        compiler_params=pltpu.CompilerParams(vmem_limit_bytes=62 * 1024 * 1024),
    )(result)


def solution(mesh):
    placed = (
        P("tm", None, "space", None, None),
        P("space", None, None),
        P("space", None, None),
        P("space", None, None),
    )
    return jax.shard_map(
        per_device,
        mesh=mesh,
        in_specs=placed,
        out_specs=P("tm", None, "space", None, None),
        check_vma=False,
    )
```

```python
import functools
import jax
import jax.numpy as jnp
from jax import lax
from jax.experimental import pallas as pl
from jax.experimental.pallas import tpu as pltpu
from jax.sharding import PartitionSpec as P

MESH = pl.DeviceIdType.MESH
SIXTH = 1.0 / 6.0
W24 = 1.0 / 24.0


def react(e, t):
    return 2.0 * e * (1.0 - e) * (e - t)


def near(v, axis, by):
    if axis == 0:
        rows, lanes = v.shape
        groups = v.reshape(rows // 8, 8, lanes)
        at = lax.broadcasted_iota(jnp.int32, groups.shape, 1)
        none = jnp.zeros((1, 8, lanes), v.dtype)
        low = pltpu.roll(groups, by, 1)
        low = jnp.where(at < by, jnp.concatenate([none, low[:-1]], axis=0), low)
        high = pltpu.roll(groups, 8 - by, 1)
        high = jnp.where(at >= 8 - by, jnp.concatenate([high[1:], none], axis=0), high)
        return (low + high).reshape(rows, lanes)
    n = v.shape[axis]
    at = lax.broadcasted_iota(jnp.int32, v.shape, axis)
    low = jnp.where(at < by, 0.0, pltpu.roll(v, by, axis))
    high = jnp.where(at >= n - by, 0.0, pltpu.roll(v, n - by, axis))
    return low + high


def tiles(v, by):
    rows, lanes = v.shape
    return pltpu.roll(v.reshape(rows // 8, 8, lanes), by, 1).reshape(rows, lanes)


def even_rows(v):
    return lax.broadcasted_iota(jnp.int32, v.shape, 0) % 2 == 0


def pair(v):
    return v + jnp.where(even_rows(v), tiles(v, 7), tiles(v, 1))


def fold(v):
    half = v.shape[0] // 2
    return jnp.where(even_rows(v[:half]), v[:half], v[half:])


def expand(x):
    even = even_rows(x)
    return jnp.where(even, x, tiles(x, 1)), jnp.where(even, tiles(x, 7), x)


def unfold(x):
    return jnp.concatenate(expand(x), axis=0)


def inplane(e):
    return near(e, 0, 1) + near(e, 1, 1) - 6.0 * e


MESSAGES = {
    name: at
    for at, name in enumerate(
        [
            (kind, side)
            for kind in ("q", "c", "n1p", "n2", "dp", "n2x", "j", "jx", "m1", "m2p", "dw", "t1", "c2")
            for side in (0, 1)
        ]
        + [(kind, side) for kind in ("n2r", "n2e", "jt") for side in (0, 1, 2)]
    )
}


def kernel(
    start, cond, thr, rec, out,
    qe, qr, c, t, k, cc, tc, kc,
    f0e, f0r, n1e, n1r, n2e, n2r, t1e, t1r,
    dE, dR, jE, jR, u1e, u2e, s1e, s1r, s2e, s2r,
    qne, qnr, m1e, m1r, m2e, m2r, t0e, t0r, oe, orr,
    n1s, n1h, ds, dh, js, jh, jxh, n2xh, rn2r, rn2e, jts, jth,
    m2s, m2h, dws, dwh, t1h, c2h,
    load_sem, store_sem, send_sem, recv_sem,
):
    nx = qr.shape[0]
    cn = nx // 2
    p, s = lax.axis_index("tm"), lax.axis_index("space")
    slices, slabs = lax.axis_size("tm"), lax.axis_size("space")
    head = p == 0
    has = (s > 0, s < slabs - 1)
    earlier, later = p > 0, p < slices - 1
    plane = qe.shape[1:]
    zeros = jnp.zeros(plane, jnp.float32)

    loads = [
        pltpu.make_async_copy(src, dst, load_sem.at[i])
        for i, (src, dst) in enumerate(
            [
                (start.at[0, 0], qe.at[pl.ds(1, nx)]),
                (cond, c.at[pl.ds(1, nx)]),
                (thr, t),
                (start.at[0, 1], qr),
                (rec, k),
            ]
        )
    ]
    for load in loads:
        load.start()

    barrier = pltpu.get_barrier_semaphore()

    def greet(when, dp, dside):
        @pl.when(when)
        def _():
            pl.semaphore_signal(barrier, inc=1, device_id=(p + dp, s + dside), device_id_type=MESH)

    greet(has[0], 0, -1)
    greet(has[1], 0, 1)
    greet(earlier, -1, 0)
    greet(earlier & has[0], -1, -1)
    greet(earlier & has[1], -1, 1)

    for side in (0, 1):
        end = side * (nx + 1)

        @pl.when(jnp.logical_not(has[side]))
        def _():
            for ref in (qe, c):
                ref[end] = zeros
            for ref in (n1h, n2xh, m2h, t1h, c2h):
                ref[side] = zeros
            n2e[end] = zeros
            m1e[end] = zeros
            for ref in (dh, jh, jxh, dwh):
                ref[side] = zeros[: plane[0] // 2]

    sides = has[0].astype(jnp.int32) + has[1].astype(jnp.int32)
    after = later.astype(jnp.int32)
    pl.semaphore_wait(barrier, sides + after * (sides + 1))

    pending = []

    def copy_of(name, src, dst, dp, dside):
        at = MESSAGES[name]
        return pltpu.make_async_remote_copy(
            src_ref=src,
            dst_ref=dst,
            send_sem=send_sem.at[at],
            recv_sem=recv_sem.at[at],
            device_id=(p + dp, s + dside),
            device_id_type=MESH,
        )

    def send(name, src, dst, when, dp=0, dside=0):
        @pl.when(when)
        def _():
            copy_of(name, src, dst, dp, dside).start()

        pending.append((name, src, dst, when, dp, dside))

    def receive(name, dst, when):
        @pl.when(when)
        def _():
            copy_of(name, dst, dst, 0, 0).wait_recv()

    def to_sides(kind, src, dst):
        for side in (0, 1):
            send((kind, side), src(side), dst(1 - side), has[side], 0, 2 * side - 1)

    def to_later_sides(kind, src, dst):
        for side in (0, 1):
            send((kind, side), src(side), dst(1 - side), later & has[side], 1, 2 * side - 1)

    def from_side(kind, side, dst, when=None):
        receive((kind, 1 - side), dst, has[side] if when is None else when & has[side])

    def edge(side):
        return side * (nx - 1)

    def halo(ref):
        return lambda side: ref.at[side * (ref.shape[0] - 1)]

    def slot(ref):
        return lambda side: ref.at[side]

    def each(low, high, body):
        for i in range(low, high):
            body(i)

    def on_edges(body):
        each(0, 2, lambda side: body(side, side * (nx - 1), 2 + side * (nx - 3)))

    to_sides("q", lambda side: start.at[0, 0, edge(side)], halo(qe))
    to_sides("c", lambda side: cond.at[edge(side)], halo(c))
    for load in loads:
        load.wait()

    def first_edge(side, i, inner):
        e, r = qe[i + 1], qr[i]
        f = c[i + 1] * (qe[inner] + inplane(e)) + react(e, t[i]) - r
        g = k[i] * (e - 0.5 * r)
        f0e[i], f0r[i] = f, g
        n1 = e + 0.5 * f
        n1e[i + 1], n1s[side], n1r[i] = n1, n1, r + 0.5 * g

    on_edges(first_edge)
    to_sides("n1p", slot(n1s), slot(n1h))

    def slow_step(i):
        g = k[i] * (n1e[i + 1] - 0.5 * n1r[i])
        t1r[i] = g
        n2r[i] = n1r[i] + 0.5 * g

    def first_inner(i):
        e, r = qe[i + 1], qr[i]
        f = c[i + 1] * (qe[i] + qe[i + 2] + inplane(e)) + react(e, t[i]) - r
        g = k[i] * (e - 0.5 * r)
        f0e[i], f0r[i] = f, g
        n1e[i + 1], n1r[i] = e + 0.5 * f, r + 0.5 * g
        slow_step(i)

    each(1, nx - 1, first_inner)

    def hand_over(kind, part, ref, shift, dst, low, count):
        src = ref.at[pl.ds(low + shift, count)]
        send((kind, part), src, dst.at[pl.ds(low, count)], later, 1)

    hand_over("n2r", 2, n2r, 0, rn2r, 1, nx - 2)

    def second(i):
        e = n1e[i + 1]
        f = c[i + 1] * (n1e[i] + n1e[i + 2] + inplane(e)) + react(e, t[i]) - n1r[i]
        t1e[i] = f
        n2e[i + 1] = e + 0.5 * f

    each(2, nx - 2, second)
    hand_over("n2e", 2, n2e, 1, rn2e, 2, nx - 4)

    def coarse_coeffs(j):
        for fine, shift, coarse in ((c, 1, cc), (t, 0, tc), (k, 0, kc)):
            coarse[j] = 0.25 * pair(fine[2 * j + shift] + fine[2 * j + 1 + shift])

    each(0, cn, coarse_coeffs)

    for side in (0, 1):
        i, end = edge(side), side * (nx + 1)
        from_side("q", side, qe.at[end])
        from_side("c", side, c.at[end])
        from_side("n1p", side, n1h.at[side])
        more = c[i + 1] * qe[end]
        f0e[i] += more
        n1e[i + 1] += 0.5 * more
        n1e[end] = n1h[side] + 0.5 * c[end] * qe[i + 1]
        slow_step(i)

    on_edges(lambda side, i, inner: second(i))
    own_edge = lambda ref: lambda side: ref.at[edge(side) + 1]
    to_sides("n2", own_edge(n2e), halo(n2e))
    on_edges(lambda side, i, inner: second(inner - 1))
    for side in (0, 1):
        hand_over("n2e", side, n2e, 1, rn2e, side * (nx - 2), 2)
        hand_over("n2r", side, n2r, 0, rn2r, edge(side), 1)

    def third(j, e_ref, r_ref, extra, missing=None):
        sums = [0.0, 0.0, 0.0, 0.0]
        for row in (0, 1):
            i = 2 * j + row
            e, r = e_ref[i + 1], r_ref[i]
            if missing == 0 and row == 0:
                x = e_ref[i + 2]
            elif missing == 1 and row == 1:
                x = e_ref[i]
            else:
                x = e_ref[i] + e_ref[i + 2]
            fe = c[i + 1] * (x + inplane(e)) + react(e, t[i]) - r
            fr = k[i] * (e - 0.5 * r)
            a, b, g, h = extra(i)
            sums[0] += a - W24 * fe
            sums[1] += b - W24 * fr
            sums[2] += g + SIXTH * fe
            sums[3] += h + SIXTH * fr
        dE[j + 1] = 0.25 * pair(sums[0])
        dR[j] = 0.25 * pair(sums[1])
        jE[j] = 0.25 * pair(sums[2])
        jR[j] = 0.25 * pair(sums[3])

    def extra_first(i):
        a, b, g, h = f0e[i], t1e[i], f0r[i], t1r[i]
        return (
            8 * W24 * b - 7 * W24 * a,
            8 * W24 * h - 7 * W24 * g,
            SIXTH * b - 2 * SIXTH * a,
            SIXTH * h - 2 * SIXTH * g,
        )

    for side in (0, 1):
        third(side * (cn - 1), n2e, n2r, extra_first, side)
        ds[side] = fold(dE[side * (cn - 1) + 1])
    to_sides("dp", slot(ds), slot(dh))
    to_later_sides("n2x", own_edge(n2e), slot(n2xh))
    each(1, cn - 1, lambda j: third(j, n2e, n2r, extra_first))

    def coarse_step(j, node, x):
        d, dr = dE[j + 1], dR[j]
        lap = 0.25 * (x + near(d, 0, 2)) + near(d, 1, 1) - 3.0 * d
        b = 0.25 * pair(node[2 * j + 1] + node[2 * j + 2])
        return 0.5 * (cc[j] * lap + react(b + d, tc[j]) - react(b, tc[j]) - dr)

    def coarse_slow(j):
        return jR[j] + 0.5 * kc[j] * (dE[j + 1] - 0.5 * dR[j])

    def coarse_first(j):
        e = jE[j] + coarse_step(j, n1e, dE[j] + dE[j + 2])
        r = coarse_slow(j)
        jE[j], jR[j] = e, r
        jts[j] = jnp.where(even_rows(e), e, r)

    each(1, cn - 1, coarse_first)
    send(("jt", 2), jts.at[pl.ds(1, cn - 2)], jth.at[pl.ds(1, cn - 2)], later, 1)

    for side in (0, 1):
        i, j, end = edge(side), side * (cn - 1), side * (nx + 1)
        from_side("n2", side, n2e.at[end])
        from_side("dp", side, dh.at[side])
        more = 0.25 * pair(c[i + 1] * n2e[end])
        change = W24 * more
        dE[j + 1] -= change
        beside = 1 + side * (cn - 3)
        jE[beside] -= 0.125 * cc[beside] * change
        jE[j] += SIXTH * more
        dE[side * (cn + 1)] = unfold(dh[side]) - (0.25 * W24) * pair(c[end] * n2e[i + 1])

    each(0, 2, lambda side: coarse_first(side * (cn - 1)))
    for side in (0, 1):
        js[side] = fold(jE[side * (cn - 1)])
    to_sides("j", slot(js), slot(jh))
    to_later_sides("jx", slot(js), slot(jxh))
    for side in (0, 1):
        last = pl.ds(side * (cn - 1), 1)
        send(("jt", side), jts.at[last], jth.at[last], later, 1)

    to_sides("t1", lambda side: thr.at[edge(side)], slot(t1h))
    to_sides("c2", lambda side: cond.at[1 + side * (nx - 3)], slot(c2h))

    def correct(j):
        for row in (0, 1):
            i = 2 * j + row
            u1e[i + 1] = n1e[i + 1] + dE[j + 1]
            u2e[i + 1] = n2e[i + 1] + jE[j]

    each(0, cn, correct)
    for side in (0, 1):
        end = side * (nx + 1)
        u1e[end] = n1e[end] + dE[side * (cn + 1)]
        u2e[end] = zeros

    def old_terms(j):
        for row in (0, 1):
            i = 2 * j + row
            u1, u2 = u1e[i + 1], u2e[i + 1]
            u1r, u2r = n1r[i] + dR[j], n2r[i] + jR[j]
            a1 = c[i + 1] * (u1e[i] + u1e[i + 2] + inplane(u1)) + react(u1, t[i]) - u1r
            a2 = c[i + 1] * (u2e[i] + u2e[i + 2] + inplane(u2)) + react(u2, t[i]) - u2r
            b1 = k[i] * (u1 - 0.5 * u1r)
            b2 = k[i] * (u2 - 0.5 * u2r)
            a0, b0 = f0e[i], f0r[i]
            s1e[i] = 8 * W24 * a1 - 7 * W24 * a0 - W24 * a2
            s1r[i] = 8 * W24 * b1 - 7 * W24 * b0 - W24 * b2
            s2e[i] = 5 * W24 * a2 - W24 * a0 - 4 * W24 * a1
            s2r[i] = 5 * W24 * b2 - W24 * b0 - 4 * W24 * b1

    each(0, cn, old_terms)

    for side in (0, 1):
        i, end = edge(side), side * (nx + 1)
        from_side("j", side, jh.at[side])
        more = c[i + 1] * (n2e[end] + unfold(jh[side]))
        s1e[i] -= W24 * more
        s2e[i] += 5 * W24 * more

    receive(("n2r", 2), rn2r.at[pl.ds(1, nx - 2)], earlier)
    receive(("n2e", 2), rn2e.at[pl.ds(2, nx - 4)], earlier)
    for side in (0, 1):
        receive(("n2r", side), rn2r.at[pl.ds(edge(side), 1)], earlier)
        receive(("n2e", side), rn2e.at[pl.ds(side * (nx - 2), 2)], earlier)
    for side in (0, 1):
        from_side("n2x", side, n2xh.at[side], earlier)
        from_side("jx", side, jxh.at[side], earlier)
        end = side * (nx + 1)
        qne[end] = jnp.where(head, qe[end], n2xh[side] + unfold(jxh[side]))
    receive(("jt", 2), jth.at[pl.ds(1, cn - 2)], earlier)
    for side in (0, 1):
        receive(("jt", side), jth.at[pl.ds(side * (cn - 1), 1)], earlier)

    def arrive(j, side=None):
        e, r = expand(jth[j])
        if side is not None:
            e -= (0.125 * W24 * 0.25) * cc[j] * pair(c[edge(side) + 1] * n2xh[side])
        for row in (0, 1):
            i = 2 * j + row
            qne[i + 1] = jnp.where(head, qe[i + 1], rn2e[i] + e)
            qnr[i] = jnp.where(head, qr[i], rn2r[i] + r)

    each(0, 2, lambda side: arrive(side * (cn - 1)))
    for side in (0, 1):
        arrive(1 + side * (cn - 3), side)
    each(2, cn - 2, arrive)

    def next_first(i):
        e, r = qne[i + 1], qnr[i]
        f = c[i + 1] * (qne[i] + qne[i + 2] + inplane(e)) + react(e, t[i]) - r
        g = k[i] * (e - 0.5 * r)
        t0e[i], t0r[i] = f, g
        m1e[i + 1] = e + 0.5 * f + s1e[i]
        m1r[i] = r + 0.5 * g + s1r[i]

    on_edges(lambda side, i, inner: next_first(i))
    to_sides("m1", own_edge(m1e), halo(m1e))
    on_edges(lambda side, i, inner: next_first(inner - 1))

    def next_second(i, x):
        e, r = m1e[i + 1], m1r[i]
        f = c[i + 1] * (x + inplane(e)) + react(e, t[i]) - r
        g = k[i] * (e - 0.5 * r)
        t1e[i], t1r[i] = f, g
        m2 = e + 0.5 * f + s2e[i]
        m2e[i + 1] = m2
        m2r[i] = r + 0.5 * g + s2r[i]
        return m2

    def next_edge(side, i, inner):
        m2s[side] = next_second(i, m1e[inner])

    on_edges(next_edge)
    to_sides("m2p", slot(m2s), slot(m2h))
    each(2, nx - 2, next_first)
    for i in sorted({1, 2, nx - 3, nx - 2}):
        next_second(i, m1e[i] + m1e[i + 2])

    def defect(i):
        return 8 * W24 * t1e[i] - 7 * W24 * t0e[i] - s1e[i]

    def next_defect(side, i, inner):
        second, third_at = inner - 1, 2 + side * (nx - 5)
        e = m2e[second + 1]
        rest = c[second + 1] * (m2e[third_at + 1] + inplane(e)) + react(e, t[second])
        rest = rest - m2r[second] - m2r[i] + c[i + 1] * e
        dws[side] = fold(0.25 * pair(defect(i) + defect(second) - W24 * rest))

    on_edges(next_defect)
    to_sides("dw", slot(dws), slot(dwh))
    each(3, nx - 3, lambda i: next_second(i, m1e[i] + m1e[i + 2]))

    for side in (0, 1):
        i, end = edge(side), side * (nx + 1)
        from_side("m1", side, m1e.at[end])
        from_side("m2p", side, m2h.at[side])
        more = c[i + 1] * m1e[end]
        t1e[i] += more
        m2e[i + 1] += 0.5 * more
        m2e[end] = m2h[side] + 0.5 * c[end] * m1e[i + 1]

    stores = []

    def store(src, dst):
        stores.append(pltpu.make_async_copy(src, dst, store_sem.at[len(stores)]))
        stores[-1].start()

    def extra_next(i):
        a, b, g, h = t0e[i], t1e[i], t0r[i], t1r[i]
        return (
            8 * W24 * b - 7 * W24 * a - s1e[i],
            8 * W24 * h - 7 * W24 * g - s1r[i],
            SIXTH * b - 2 * SIXTH * a - s1e[i] - s2e[i],
            SIXTH * h - 2 * SIXTH * g - s1r[i] - s2r[i],
        )

    each(0, cn, lambda j: third(j, m2e, m2r, extra_next))

    def final_slow(j):
        r = coarse_slow(j)
        for row in (0, 1):
            orr[2 * j + row] = m2r[2 * j + row] + r

    each(0, cn, final_slow)
    store(orr, out.at[0, 1])

    def final_fast(j):
        e = jE[j] + coarse_step(j, m1e, dE[j] + dE[j + 2])
        for row in (0, 1):
            oe[2 * j + row] = m2e[2 * j + 1 + row] + e

    def store_fast(low, count):
        rows = pl.ds(low, count)
        store(oe.at[rows], out.at[0, 0, rows])

    each(1, cn - 1, final_fast)
    store_fast(2, nx - 4)

    for side in (0, 1):
        i, end = edge(side), side * (nx + 1)
        from_side("dw", side, dwh.at[side])
        from_side("t1", side, t1h.at[side])
        from_side("c2", side, c2h.at[side])
        own, beyond = m2e[i + 1], m2e[end]
        rest = c[end] * (own + inplane(beyond)) + react(beyond, t1h[side]) + c2h[side] * beyond
        more = 8 * W24 * c[end] * m1e[i + 1] - W24 * rest
        dE[side * (cn + 1)] = unfold(dwh[side]) + 0.25 * pair(more)
        final_fast(side * (cn - 1))
        store_fast(side * (nx - 2), 2)

    for name, src, dst, when, dp, dside in pending:

        @pl.when(when)
        def _():
            copy_of(name, src, dst, dp, dside).wait_send()

    for stored in stores:
        stored.wait()


def per_device(start, conduct, threshold, recovery):
    nx, ny, nz = conduct.shape
    cn = nx // 2

    def planes(count, rows=ny):
        return pltpu.VMEM((count, rows, nz), jnp.float32)

    own, padded, coarse, two, half = (
        planes(nx), planes(nx + 2), planes(cn), planes(2), planes(2, ny // 2)
    )
    scratch = [
        padded, own, padded, own, own, coarse, coarse, coarse,
        own, own, padded, own, padded, own, own, own,
        planes(cn + 2), coarse, coarse, coarse, padded, padded, own, own, own, own,
        padded, own, padded, own, padded, own, own, own, own, own,
        two, two, half, half, half, half, half, two, own, own, coarse, coarse,
        two, two, half, half, two, two,
        pltpu.SemaphoreType.DMA((5,)),
        pltpu.SemaphoreType.DMA((6,)),
        pltpu.SemaphoreType.DMA((len(MESSAGES),)),
        pltpu.SemaphoreType.DMA((len(MESSAGES),)),
    ]
    return pl.pallas_call(
        kernel,
        out_shape=jax.ShapeDtypeStruct(start.shape, jnp.float32),
        in_specs=[pl.BlockSpec(memory_space=pl.ANY)] * 4,
        out_specs=pl.BlockSpec(memory_space=pl.ANY),
        scratch_shapes=scratch,
        compiler_params=pltpu.CompilerParams(
            collective_id=0, has_side_effects=True, vmem_limit_bytes=62 * 1024 * 1024
        ),
    )(start, conduct, threshold, recovery)


def solution(mesh):
    placed = (
        P("tm", None, "space", None, None),
        P("space", None, None),
        P("space", None, None),
        P("space", None, None),
    )
    return jax.shard_map(
        per_device,
        mesh=mesh,
        in_specs=placed,
        out_specs=P("tm", None, "space", None, None),
        check_vma=False,
    )
```
